512 devices in a mesh: train: 32 (over z, x_lo, core), query: 16 (over x_hi, y).
Axes of the slice: x: 4 (x_hi: 2, x_lo: 2; x = x_hi * 2 + x_lo), y: 8, z: 8, core: 2. Of those that a mesh axis runs over, the one named last changes fastest.
Arguments:
- train_factors: bfloat16 [16384, 2, 256, 128], P(('train', 'query')), may hold values from -6 to 6
- train_lengths: int32 [16384], P(('train', 'query')), may hold values from 64 to 256, as said below
- query_factors: bfloat16 [128, 2, 8192, 128], P('query', None, 'train'), may hold values from -6 to 6
- query_lengths: int32 [128], P('query'), may hold values from 4097 to 8192, as said below
- basis_out: float32 [2, 64, 64], replicated, may hold values from -0.75 to 0.75
- basis_in: float32 [2, 64, 64], replicated, may hold values from -0.75 to 0.75
- eigenvalues: float32 [2, 64, 64], replicated, may hold values from 0.1 to 10
Outputs:
- scores: float32 [16384, 128], P('train', 'query')
The draws below stay inside these ranges and needn't reach their ends.
Inputs may be any that keep to these rules, and one draw needn't show every extreme that they name: `train_lengths`: each train document has 256 live tokens or fewer, and some document in every draw has exactly 256; some has exactly 64. `query_lengths`: each query document has more than half of its 8192 slots live; some document in every draw has all 8192, and some has exactly 4097.
All inputs are finite; a program needn't handle non-finite values.
Results may differ from the reference program's by a relative error of at most 0.0035.
Values may be sent and summed in bfloat16 or wider, within the bound.
A program may use at most 64 MiB of HBM per device.

```python
import math
import jax
import jax.numpy as jnp
from jax import lax

RANK = 64
LAYERS = 2
TR_LEN = 256
TR_DEV = 32
QLEN = 8192
NTRAIN = 16384
NQUERY = 128


def draw_train_lengths(key, part):
    key = jax.random.fold_in(key, 11)
    values = jax.random.randint(key, (NTRAIN,), TR_LEN // 4, TR_LEN + 1)
    places = jnp.arange(NTRAIN) % 8
    values = jnp.where(places == 0, TR_LEN, values)
    values = jnp.where(places == 3, TR_LEN // 4, values)
    return values.astype(jnp.int32)


def draw_query_lengths(key, part):
    key = jax.random.fold_in(key, 23)
    values = jax.random.randint(key, (NQUERY,), QLEN // 2 + 1, QLEN + 1)
    places = jnp.arange(NQUERY) % 4
    values = jnp.where(places == 0, QLEN, values)
    values = jnp.where(places == 1, QLEN // 2 + 1, values)
    return values.astype(jnp.int32)


def block_scale(key, shape, cuts, smallest, top_value):
    gain, own = 1.0, jax.random.fold_in(key, 6)
    for position, parts in cuts:
        steps = jnp.exp(jax.random.uniform(jax.random.fold_in(own, position), (parts,), jnp.float32, smallest / len(cuts), top_value / len(cuts)))
        gain = gain * jnp.repeat(steps, shape[position] // parts).reshape([-1 if axis == position else 1 for axis in range(len(shape))])
    return gain


def normal_values(rng, dims, scale, most, split=(), kind=jnp.bfloat16):
    result = jax.random.normal(rng, dims, jnp.float32) * scale
    if len(split) > 0:
        result = block_scale(rng, dims, split, -0.22, 0.18) * result
    return jnp.clip(result, min=-most, max=most).astype(kind)


def setup_inputs(seed: int = 0) -> dict:
    seeds = jax.random.split(jax.random.key(seed), 8)
    train_factors = normal_values(seeds[0], (NTRAIN, LAYERS, TR_LEN, 2 * RANK), 1.0, 6.0, ((0, 512),))
    train_lengths = draw_train_lengths(jax.random.fold_in(seeds[7], 71), 0)
    query_factors = normal_values(seeds[2], (NQUERY, LAYERS, QLEN, 2 * RANK), 1.0, 6.0, ((0, 16), (2, 32)))
    query_lengths = draw_query_lengths(jax.random.fold_in(seeds[7], 71), 0)
    basis_out = normal_values(seeds[4], (LAYERS, RANK, RANK), RANK ** -0.5, 0.75, (), jnp.float32)
    basis_in = normal_values(seeds[5], (LAYERS, RANK, RANK), RANK ** -0.5, 0.75, (), jnp.float32)
    eigenvalues = jnp.clip(jnp.exp(jax.random.uniform(seeds[6], (LAYERS, RANK, RANK), jnp.float32, math.log(0.1), math.log(10.0))), 0.1, 10.0)
    return {"train_factors": train_factors, "train_lengths": train_lengths, "query_factors": query_factors, "query_lengths": query_lengths, "basis_out": basis_out, "basis_in": basis_in, "eigenvalues": eigenvalues}


def outer_sums(factors, lengths, slots, token_norm):
    live_mask = (jnp.arange(slots)[None, :] < lengths[:, None]).astype(jnp.float32)
    activations = factors[..., :RANK].astype(jnp.float32)
    gradients = factors[..., RANK:].astype(jnp.float32) * live_mask[:, None, :, None]
    summed = jnp.einsum('dltr,dlts->dlrs', gradients, activations, precision=lax.Precision.HIGHEST)
    return summed * token_norm

def rotate(summed, basis_out, basis_in, inv_root):
    half_turn = jnp.einsum('lra,dlrs->dlas', basis_out, summed, precision=lax.Precision.HIGHEST)
    rotated = jnp.einsum('dlas,lsb->dlab', half_turn, basis_in, precision=lax.Precision.HIGHEST)
    rotated = rotated * inv_root[None]
    return rotated.reshape(rotated.shape[0], -1).astype(jnp.bfloat16)

def reference(train_factors, train_lengths, query_factors, query_lengths, basis_out, basis_in, eigenvalues):
    inv_root = 1.0 / jnp.sqrt(eigenvalues)
    query_slots = query_factors.shape[2]
    query_norm = 1.0 / math.sqrt(query_slots)
    train_norm = 1.0 / math.sqrt(TR_LEN)
    score_norm = 1.0 / (RANK * math.sqrt(LAYERS))

    def one_query(packed):
        factors, lengths = packed
        summed = outer_sums(factors, lengths, query_slots, query_norm)
        return rotate(summed, basis_out, basis_in, inv_root)
    query_blocks = query_factors.reshape(NQUERY, 1, LAYERS, query_slots, 2 * RANK)
    query_rotated = lax.map(one_query, (query_blocks, query_lengths.reshape(NQUERY, 1)))
    query_rotated = query_rotated.reshape(NQUERY, -1)
    block_count = NTRAIN // TR_DEV

    def one_block(packed):
        factors, lengths = packed
        summed = outer_sums(factors, lengths, TR_LEN, train_norm)
        train_rotated = rotate(summed, basis_out, basis_in, inv_root)
        product = lax.dot_general(train_rotated, query_rotated, (((1,), (1,)), ((), ())), preferred_element_type=jnp.float32)
        return product * score_norm
    train_blocks = train_factors.reshape(block_count, TR_DEV, LAYERS, TR_LEN, 2 * RANK)
    scores = lax.map(one_block, (train_blocks, train_lengths.reshape(block_count, TR_DEV)))
    return scores.reshape(NTRAIN, NQUERY)
```

```python
import functools
import math

import jax
import jax.numpy as jnp
from jax import lax
from jax.experimental import pallas as pl
from jax.experimental.pallas import tpu as pltpu
from jax.sharding import PartitionSpec as P

F32 = jnp.float32
BF16 = jnp.bfloat16
MESH = pl.DeviceIdType.MESH


def split(value):
    high = value.astype(BF16)
    return high, (value - high.astype(F32)).astype(BF16)


def mm(lhs, rhs):
    return jnp.dot(lhs, rhs, preferred_element_type=F32)


def kernel(
    nz, ny, score_norm, train_norm, query_norm,
    train_hbm, train_len, query_hbm, query_len, basis_out, basis_in, eigenvalues,
    out_ref,
    train_buf, query_buf, right_ref, left_ref, scale_ref,
    partial, sibling_part, pieces, gathered, rotated, score_send, score_recv,
    load_sem, query_sem, pair_sem, reduce_sem, plane_sem, ring_sem, ring_send_sem, sib_sem, score_sem,
):
    rank = basis_in.shape[1]
    lanes = 2 * rank
    train_docs = train_hbm.shape[0]
    query_docs = query_hbm.shape[0]
    slots = train_hbm.shape[2]
    pairs = nz * 2
    plane = ny * 4
    groups = ny * 2
    chunk = plane
    half = chunk // 2
    chunks = nz

    train = lax.axis_index("train")
    query = lax.axis_index("query")
    z = train // 4
    x_lo = (train // 2) % 2
    core = train % 2
    x_hi = query // ny
    y = query % ny
    pair = train // 2
    c = core * y + (1 - core) * z
    d = core * z + (1 - core) * y
    spot = d * 4 + x_lo * 2 + x_hi

    sibling = (train + 1 - 2 * core, query)

    def reduce_partner(j):
        other = (pair + j) % pairs
        return other, (other * 2 + core, query)

    def plane_partner(j):
        other = (spot + j) % plane
        od = other // 4
        oxl = (other // 2) % 2
        oxh = other % 2
        oz = core * od + (1 - core) * z
        oy = core * y + (1 - core) * od
        return oz * 4 + oxl * 2 + core, oxh * ny + oy

    def ring_partner(step):
        oc = (c + step + chunks) % chunks
        oz = core * z + (1 - core) * oc
        oy = core * oc + (1 - core) * y
        return oz * 4 + x_lo * 2 + core, x_hi * ny + oy

    def score_partner(j):
        other = (query + j) % groups
        return other, (train, other)

    load_query = pltpu.make_async_copy(query_hbm, query_buf, query_sem)
    load_query.start()
    loads = []
    parts = load_sem.shape[0]
    part_docs = train_docs // parts
    for i in range(parts):
        window = pl.ds(i * part_docs, part_docs)
        loads.append(pltpu.make_async_copy(train_hbm.at[window], train_buf.at[window], load_sem.at[i]))
        loads[-1].start()

    barrier = pltpu.get_barrier_semaphore()
    pl.semaphore_signal(barrier, inc=1, device_id=sibling, device_id_type=MESH)

    def greet_reduce(j, carry):
        pl.semaphore_signal(barrier, inc=1, device_id=reduce_partner(j)[1], device_id_type=MESH)
        return carry

    def greet_plane(j, carry):
        pl.semaphore_signal(barrier, inc=1, device_id=plane_partner(j), device_id_type=MESH)
        return carry

    def greet_score(j, carry):
        pl.semaphore_signal(barrier, inc=1, device_id=score_partner(j)[1], device_id_type=MESH)
        return carry

    lax.fori_loop(1, pairs, greet_reduce, 0)
    lax.fori_loop(1, plane, greet_plane, 0)
    lax.fori_loop(1, groups, greet_score, 0)
    for step in (1, -1):
        pl.semaphore_signal(barrier, inc=1, device_id=ring_partner(step), device_id_type=MESH)
    greetings = 1 + (pairs - 1) + (plane - 1) + (groups - 1) + 2

    zero = jnp.zeros((rank, rank), F32)
    block = jnp.concatenate(
        [
            jnp.concatenate([basis_in[0], zero], axis=1),
            jnp.concatenate([zero, basis_in[1]], axis=1),
        ],
        axis=0,
    )
    high, low = split(block)
    right_ref[...] = jnp.concatenate([high, high, low], axis=0)
    turned = jnp.concatenate([basis_out[0].T, basis_out[1].T], axis=0)
    high, low = split(turned)
    left_ref[...] = jnp.concatenate([high, high, low], axis=1)
    scale_ref[...] = 1.0 / jnp.sqrt(jnp.concatenate([eigenvalues[0], eigenvalues[1]], axis=1))

    lane = lax.broadcasted_iota(jnp.int32, (rank, lanes), 1)
    first_layer = lane < rank
    token = lax.broadcasted_iota(jnp.int32, (slots, lanes), 0)

    def outer(factors, live):
        mask = jnp.where(token < live, 1.0, 0.0).astype(BF16)
        sums = []
        for layer in range(2):
            tokens = factors[layer]
            masked = tokens * mask
            product = lax.dot_general(
                masked, tokens, (((0,), (0,)), ((), ())), preferred_element_type=F32
            )
            sums.append(product[rank:])
        return jnp.where(first_layer, sums[0], pltpu.roll(sums[1], rank, 1))

    def rotate(summed, norm):
        count = len(summed)
        high, low = split(jnp.concatenate(summed, axis=0))
        turned = mm(jnp.concatenate([high, low, high], axis=1), right_ref[...])
        high, low = split(turned)
        columns = []
        for i in range(count):
            rows = slice(i * rank, (i + 1) * rank)
            columns.append(jnp.concatenate([high[rows], low[rows], high[rows]], axis=0))
        product = mm(left_ref[...], jnp.concatenate(columns, axis=1))
        scale = scale_ref[...] * norm
        results = []
        for i in range(count):
            mine = product[:, i * lanes:(i + 1) * lanes]
            results.append(jnp.where(first_layer, mine[:rank], mine[rank:]) * scale)
        return results

    load_query.wait()
    query_batch = 4

    def query_step(step, carry):
        summed = []
        for i in range(query_batch):
            doc = step * query_batch + i
            summed.append(outer(query_buf[doc], query_len[doc] - train * slots))
        for i, value in enumerate(rotate(summed, query_norm)):
            partial[:, pl.ds(step * query_batch + i, 1), :] = value[:, None, :]
        return carry

    lax.fori_loop(0, query_docs // query_batch, query_step, 0)

    pl.semaphore_wait(barrier, greetings)
    half_rows = rank // 2
    pair_copy = pltpu.make_async_remote_copy(
        src_ref=partial.at[pl.ds((1 - core) * half_rows, half_rows)],
        dst_ref=sibling_part,
        send_sem=pair_sem.at[0],
        recv_sem=pair_sem.at[1],
        device_id=sibling,
        device_id_type=MESH,
    )
    pair_copy.start()

    train_batch = 4
    per_part = part_docs // train_batch

    def train_step(step, carry):
        summed = []
        for i in range(train_batch):
            doc = step * train_batch + i
            summed.append(outer(train_buf[doc], train_len[doc]))
        for i, value in enumerate(rotate(summed, train_norm)):
            rotated[:, pl.ds(step * train_batch + i, 1), :] = value[:, None, :]
        return carry

    def train_part(i):
        loads[i].wait()
        lax.fori_loop(i * per_part, (i + 1) * per_part, train_step, 0)

    pair_copy.wait()
    sibling_part[...] = sibling_part[...] + partial[pl.ds(core * half_rows, half_rows)]

    def send_reduce(j, carry):
        other, target = reduce_partner(j)
        pltpu.make_async_remote_copy(
            src_ref=sibling_part.at[pl.ds(other * 2, 2)],
            dst_ref=pieces.at[j],
            send_sem=reduce_sem.at[0],
            recv_sem=reduce_sem.at[1],
            device_id=target,
            device_id_type=MESH,
        ).start()
        return carry

    lax.fori_loop(1, pairs, send_reduce, 0)
    train_part(0)
    others = pieces.at[pl.ds(1, pairs - 1)]
    pltpu.make_async_copy(others, others, reduce_sem.at[1]).wait()
    total = sibling_part[pl.ds(pair * 2, 2)]
    for j in range(1, pairs):
        total = total + pieces[j]
    tile_rows = 2 * query_docs
    gathered[core, c * plane + spot] = total.reshape(tile_rows, lanes).astype(BF16)

    mine = gathered.at[core, c * plane + spot]

    def send_plane(j, carry):
        pltpu.make_async_remote_copy(
            src_ref=mine,
            dst_ref=mine,
            send_sem=plane_sem.at[0],
            recv_sem=plane_sem.at[1],
            device_id=plane_partner(j),
            device_id_type=MESH,
        ).start()
        return carry

    lax.fori_loop(1, plane, send_plane, 0)
    train_part(1)
    others = gathered.at[0, pl.ds(0, plane - 1)]
    pltpu.make_async_copy(others, others, plane_sem.at[1]).wait()

    steps = chunks // 2

    def window(origin, sub, count):
        return gathered.at[core, pl.ds(origin * chunk + sub * half, count)]

    def ring_copy(way, step, sub):
        origin = (c - way * (step - 1) + chunks) % chunks
        side = (1 - way) // 2
        return pltpu.make_async_remote_copy(
            src_ref=window(origin, sub, half),
            dst_ref=window(origin, sub, half),
            send_sem=ring_send_sem,
            recv_sem=ring_sem.at[side, step - 1, sub],
            device_id=ring_partner(way),
            device_id_type=MESH,
        )

    def sib_copy(origin, sub, count):
        return pltpu.make_async_remote_copy(
            src_ref=window(origin, sub, count),
            dst_ref=window(origin, sub, count),
            send_sem=sib_sem.at[0],
            recv_sem=sib_sem.at[1],
            device_id=sibling,
            device_id_type=MESH,
        )

    def wanted(way, step, sub):
        return step < steps or (step == steps and sub == (1 - way) // 2)

    for sub in range(2):
        for way in (1, -1):
            if wanted(way, 1, sub):
                ring_copy(way, 1, sub).start()
    sib_copy(c, 0, chunk).start()
    done = 2
    for step in range(1, steps + 1):
        if done < parts:
            train_part(done)
            done += 1
        for sub in range(2):
            for way in (1, -1):
                if not wanted(way, step, sub):
                    continue
                ring_copy(way, step, sub).wait_recv()
                if wanted(way, step + 1, sub):
                    ring_copy(way, step + 1, sub).start()
                sib_copy((c - way * step + chunks) % chunks, sub, half).start()
    for i in range(done, parts):
        train_part(i)
    whole = gathered.at[0]
    pltpu.make_async_copy(whole, whole, sib_sem.at[1]).wait()

    rows = groups * tile_rows

    total = jnp.zeros((rows, 2 * train_docs), F32)
    for side in range(2):
        for i in range(pairs):
            iz, ixl = i // 2, i % 2
            tiles = []
            for iy in range(ny):
                first = (iz * ny + iy if side == 0 else iy * nz + iz) * 4 + ixl * 2
                tiles.append(gathered[side, first:first + 2].reshape(2 * tile_rows, lanes))
            row = side * half_rows + 2 * i
            documents = rotated[row:row + 2].reshape(2 * train_docs, lanes).astype(BF16)
            total = total + lax.dot_general(
                jnp.concatenate(tiles, axis=0), documents, (((1,), (1,)), ((), ())), preferred_element_type=F32
            )
    total = total.reshape(groups, 2, query_docs, 2 * train_docs)
    scores = (total[:, 0, :, :train_docs] + total[:, 1, :, train_docs:]) * score_norm
    share = score_recv.shape[2] // train_docs
    wide = jnp.concatenate([scores] * share, axis=2)
    lane = lax.broadcasted_iota(jnp.int32, wide.shape, 2)
    place = query % share
    score_send[...] = jnp.where((lane >= place * train_docs) & (lane < (place + 1) * train_docs), wide, 0.0)

    def send_scores(j, carry):
        other, target = score_partner(j)
        pltpu.make_async_remote_copy(
            src_ref=score_send.at[(other % ny) * 2 + other // ny],
            dst_ref=score_recv.at[query],
            send_sem=score_sem.at[0],
            recv_sem=score_sem.at[1],
            device_id=target,
            device_id_type=MESH,
        ).start()
        return carry

    lax.fori_loop(1, groups, send_scores, 0)
    score_recv[query] = score_send[y * 2 + x_hi]

    pltpu.make_async_copy(others, others, plane_sem.at[0]).wait()
    others = pieces.at[pl.ds(1, pairs - 1)]
    pltpu.make_async_copy(others, others, reduce_sem.at[0]).wait()
    others = gathered.at[0, pl.ds(0, (chunks - 1) * chunk)]
    pltpu.make_async_copy(others, others, ring_send_sem).wait()
    pltpu.make_async_copy(whole, whole, sib_sem.at[0]).wait()

    others = score_recv.at[pl.ds(0, groups - 1)]
    pltpu.make_async_copy(others, others, score_sem.at[1]).wait()
    for i in range(groups // share):
        value = score_recv[i * share]
        for k in range(1, share):
            value = value + score_recv[i * share + k]
        out_ref[:, i * share * train_docs:(i + 1) * share * train_docs] = value
    pltpu.make_async_copy(others, others, score_sem.at[0]).wait()


def on_device(
    train_factors, train_lengths, query_factors, query_lengths, basis_out, basis_in, eigenvalues
):
    layer_count, rank, _ = basis_in.shape
    train_docs, _, slots, lanes = train_factors.shape
    query_docs = query_factors.shape[0]
    trains = lax.axis_size("train")
    groups = lax.axis_size("query")
    nz, ny = trains // 4, groups // 2
    pairs, plane = nz * 2, ny * 4
    tile_rows = 2 * query_docs
    share = min(groups, 128 // train_docs)
    score_norm = 1.0 / (rank * math.sqrt(layer_count))
    train_norm = 1.0 / math.sqrt(slots)
    query_norm = 1.0 / math.sqrt(slots * trains)
    vmem = pl.BlockSpec(memory_space=pltpu.VMEM)
    smem = pl.BlockSpec(memory_space=pltpu.SMEM)
    hbm = pl.BlockSpec(memory_space=pl.ANY)
    dma = pltpu.SemaphoreType.DMA
    scores = pl.pallas_call(
        functools.partial(kernel, nz, ny, score_norm, train_norm, query_norm),
        out_shape=jax.ShapeDtypeStruct((query_docs, groups * train_docs), F32),
        in_specs=[hbm, smem, hbm, smem, vmem, vmem, vmem],
        out_specs=vmem,
        scratch_shapes=[
            pltpu.VMEM(train_factors.shape, BF16),
            pltpu.VMEM(query_factors.shape, BF16),
            pltpu.VMEM((3 * lanes, lanes), BF16),
            pltpu.VMEM((lanes, 3 * rank), BF16),
            pltpu.VMEM((rank, lanes), F32),
            pltpu.VMEM((rank, query_docs, lanes), F32),
            pltpu.VMEM((rank // 2, query_docs, lanes), F32),
            pltpu.VMEM((pairs, 2, query_docs, lanes), F32),
            pltpu.VMEM((2, nz * plane, tile_rows, lanes), BF16),
            pltpu.VMEM((rank, train_docs, lanes), F32),
            pltpu.VMEM((groups, query_docs, share * train_docs), F32),
            pltpu.VMEM((groups, query_docs, share * train_docs), F32),
            dma((4,)),
            dma,
            dma((2,)),
            dma((2,)),
            dma((2,)),
            dma((2, nz // 2, 2)),
            dma,
            dma((2,)),
            dma((2,)),
        ],
        compiler_params=pltpu.CompilerParams(
            collective_id=0, has_side_effects=True, vmem_limit_bytes=40 * 1024 * 1024
        ),
        cost_estimate=pl.CostEstimate(flops=400_000_000, bytes_accessed=6_000_000, transcendentals=0),
    )(
        train_factors, train_lengths, query_factors, query_lengths, basis_out, basis_in, eigenvalues
    )
    return scores.T


def solution(mesh):
    return jax.shard_map(
        on_device,
        mesh=mesh,
        in_specs=(
            P(("train", "query"), None, None, None),
            P(("train", "query")),
            P("query", None, "train", None),
            P("query"),
            P(),
            P(),
            P(),
        ),
        out_specs=P("train", "query"),
        check_vma=False,
    )
```

```python
import functools
import math

import jax
import jax.numpy as jnp
from jax import lax
from jax.experimental import pallas as pl
from jax.experimental.pallas import tpu as pltpu
from jax.sharding import PartitionSpec as P

F32 = jnp.float32
BF16 = jnp.bfloat16
MESH = pl.DeviceIdType.MESH


def split(value):
    high = value.astype(BF16)
    return high, (value - high.astype(F32)).astype(BF16)


def mm(lhs, rhs):
    return jnp.dot(lhs, rhs, preferred_element_type=F32)


def kernel(
    nz, ny, score_norm, train_norm, query_norm,
    train_hbm, train_len_hbm, query_hbm, query_len_hbm, basis_out_hbm, basis_in_hbm, eigenvalues_hbm,
    out_ref,
    train_buf, train_len, query_buf, query_len, basis_out, basis_in, eigenvalues,
    right_ref, left_ref, scale_ref,
    partial, sibling_part, pieces, gathered, rotated, rows_own, rows_all, score_send, score_recv,
    load_sem, query_sem, small_sem, pair_sem, reduce_sem, plane_sem, sib_sem, rows_sem, score_sem,
):
    rank = basis_in.shape[1]
    lanes = 2 * rank
    train_docs = train_hbm.shape[0]
    query_docs = query_hbm.shape[0]
    slots = train_hbm.shape[2]
    slab = rank // ny
    groups = ny * 2
    plane = nz * 4
    tile_rows = 2 * query_docs

    train = lax.axis_index("train")
    query = lax.axis_index("query")
    z = train // 4
    x_lo = (train // 2) % 2
    core = train % 2
    x_hi = query // ny
    y = query % ny
    spot = z * 4 + x_hi * 2 + x_lo
    tile_group = x_hi * ny + z

    def device(dz, dxl, dxh, dy):
        return dz * 4 + dxl * 2 + core, dxh * ny + dy

    sibling = (train + 1 - 2 * core, query)

    def plane_partner(j):
        other = (spot + j) % plane
        return device(other // 4, other % 2, (other // 2) % 2, y)

    def score_partner(j):
        other = (query + j) % groups
        return other, (train, other)

    load_query = pltpu.make_async_copy(query_hbm, query_buf, query_sem)
    load_query.start()
    small = [
        pltpu.make_async_copy(src, dst, small_sem.at[i])
        for i, (src, dst) in enumerate(
            [
                (query_len_hbm, query_len),
                (basis_in_hbm, basis_in),
                (basis_out_hbm, basis_out),
                (eigenvalues_hbm, eigenvalues),
                (train_len_hbm, train_len),
            ]
        )
    ]
    for copy in small:
        copy.start()
    parts = load_sem.shape[0]
    part_docs = train_docs // parts
    loads = []
    for i in range(parts):
        window = pl.ds(i * part_docs, part_docs)
        loads.append(pltpu.make_async_copy(train_hbm.at[window], train_buf.at[window], load_sem.at[i]))
        loads[-1].start()

    barrier = pltpu.get_barrier_semaphore()

    def greet(target):
        pl.semaphore_signal(barrier, inc=1, device_id=target, device_id_type=MESH)

    greet(sibling)

    def greet_reduce(j, carry):
        source = device(j // 2, j % 2, x_hi, z)
        own = (source[0] == train) & (source[1] == query)
        greet((source[0] + jnp.where(own, 1 - 2 * core, 0), source[1]))
        return carry

    def greet_plane(j, carry):
        greet(plane_partner(j))
        return carry

    def greet_score(j, carry):
        greet(score_partner(j)[1])
        return carry

    lax.fori_loop(0, nz * 2, greet_reduce, 0)
    lax.fori_loop(1, plane, greet_plane, 0)
    lax.fori_loop(1, groups, greet_score, 0)
    greetings = 1 + nz * 2 + (plane - 1) + (groups - 1)

    for copy in small:
        copy.wait()
    zero = jnp.zeros((rank, rank), F32)
    block = jnp.concatenate(
        [
            jnp.concatenate([basis_in[0], zero], axis=1),
            jnp.concatenate([zero, basis_in[1]], axis=1),
        ],
        axis=0,
    )
    high, low = split(block)
    right_ref[...] = jnp.concatenate([high, high, low], axis=0)
    turned = jnp.concatenate([basis_out[0].T, basis_out[1].T], axis=0)
    high, low = split(turned)
    left_ref[...] = jnp.concatenate([high, high, low], axis=1)
    scale_ref[...] = 1.0 / jnp.sqrt(jnp.concatenate([eigenvalues[0], eigenvalues[1]], axis=1))

    lane = lax.broadcasted_iota(jnp.int32, (rank, lanes), 1)
    first_layer = lane < rank
    token = lax.broadcasted_iota(jnp.int32, (slots, lanes), 0)

    def outer(factors, live):
        mask = jnp.where(token < live, 1.0, 0.0).astype(BF16)
        sums = []
        for layer in range(2):
            tokens = factors[layer]
            masked = tokens * mask
            product = lax.dot_general(
                masked, tokens, (((0,), (0,)), ((), ())), preferred_element_type=F32
            )
            sums.append(product[rank:])
        return jnp.where(first_layer, sums[0], pltpu.roll(sums[1], rank, 1))

    def rotate(summed, norm):
        count = len(summed)
        high, low = split(jnp.concatenate(summed, axis=0))
        turned = mm(jnp.concatenate([high, low, high], axis=1), right_ref[...])
        high, low = split(turned)
        columns = []
        for i in range(count):
            rows = slice(i * rank, (i + 1) * rank)
            columns.append(jnp.concatenate([high[rows], low[rows], high[rows]], axis=0))
        product = mm(left_ref[...], jnp.concatenate(columns, axis=1))
        scale = scale_ref[...] * norm
        results = []
        for i in range(count):
            mine = product[:, i * lanes:(i + 1) * lanes]
            results.append(jnp.where(first_layer, mine[:rank], mine[rank:]) * scale)
        return results

    load_query.wait()
    query_batch = 4

    def query_step(step, carry):
        summed = []
        for i in range(query_batch):
            doc = step * query_batch + i
            summed.append(outer(query_buf[doc], query_len[doc] - train * slots))
        for i, value in enumerate(rotate(summed, query_norm)):
            partial[:, :, :, pl.ds(step * query_batch + i, 1), :] = value.reshape(ny, 2, slab // 2, 1, lanes)
        return carry

    lax.fori_loop(0, query_docs // query_batch, query_step, 0)

    pl.semaphore_wait(barrier, greetings)
    pair_copy = pltpu.make_async_remote_copy(
        src_ref=partial.at[:, 1 - core],
        dst_ref=sibling_part,
        send_sem=pair_sem.at[0],
        recv_sem=pair_sem.at[1],
        device_id=sibling,
        device_id_type=MESH,
    )
    pair_copy.start()

    train_batch = 4
    per_part = part_docs // train_batch

    def train_step(step, carry):
        summed = []
        for i in range(train_batch):
            doc = step * train_batch + i
            summed.append(outer(train_buf[doc], train_len[doc]))
        for i, value in enumerate(rotate(summed, train_norm)):
            rotated[:, pl.ds(step * train_batch + i, 1), :] = value[:, None, :]
        return carry

    def train_part(i):
        loads[i].wait()
        lax.fori_loop(i * per_part, (i + 1) * per_part, train_step, 0)

    batches = rows_own.shape[1]
    batch_docs = train_docs // batches

    def send_rows(i):
        rows_own[:, i] = rotated[:, i * batch_docs:(i + 1) * batch_docs, :].astype(BF16)

        def send(j, carry):
            other = (y + j) % ny
            pltpu.make_async_remote_copy(
                src_ref=rows_own.at[pl.ds(other * slab, slab), i],
                dst_ref=rows_all.at[:, y, i],
                send_sem=rows_sem.at[0],
                recv_sem=rows_sem.at[1],
                device_id=device(z, x_lo, x_hi, other),
                device_id_type=MESH,
            ).start()
            return carry

        lax.fori_loop(1, ny, send, 0)
        rows_all[:, y, i] = rows_own[pl.ds(y * slab, slab), i]

    pair_copy.wait()
    sibling_part[...] = sibling_part[...] + partial[:, core]

    def send_reduce(j, carry):
        s, half = j // 2, j % 2
        target = device(y, half, x_hi, s)
        src = sibling_part.at[s, pl.ds(half * 2, 2)]
        dst = pieces.at[z * 2 + x_lo]

        @pl.when((target[0] == train) & (target[1] == query))
        def _():
            pltpu.make_async_copy(src, dst, reduce_sem.at[1]).start()

        @pl.when((target[0] != train) | (target[1] != query))
        def _():
            pltpu.make_async_remote_copy(
                src_ref=src,
                dst_ref=dst,
                send_sem=reduce_sem.at[0],
                recv_sem=reduce_sem.at[1],
                device_id=target,
                device_id_type=MESH,
            ).start()

        return carry

    lax.fori_loop(0, ny * 2, send_reduce, 0)
    train_part(0)
    train_part(1)
    send_rows(0)
    pltpu.make_async_copy(pieces, pieces, reduce_sem.at[1]).wait()
    total = pieces[0]
    for j in range(1, nz * 2):
        total = total + pieces[j]
    gathered[core, x_lo * groups + tile_group] = total.reshape(tile_rows, lanes).astype(BF16)

    mine = gathered.at[core, x_lo * groups + tile_group]

    def send_plane(j, carry):
        pltpu.make_async_remote_copy(
            src_ref=mine,
            dst_ref=mine,
            send_sem=plane_sem.at[0],
            recv_sem=plane_sem.at[1],
            device_id=plane_partner(j),
            device_id_type=MESH,
        ).start()
        return carry

    lax.fori_loop(1, plane, send_plane, 0)
    train_part(2)
    train_part(3)
    send_rows(1)
    others = gathered.at[0, pl.ds(0, plane - 1)]
    pltpu.make_async_copy(others, others, plane_sem.at[1]).wait()

    sib_copy = pltpu.make_async_remote_copy(
        src_ref=gathered.at[core],
        dst_ref=gathered.at[core],
        send_sem=sib_sem.at[0],
        recv_sem=sib_sem.at[1],
        device_id=sibling,
        device_id_type=MESH,
    )
    sib_copy.start()
    received = rows_all.at[:, pl.ds(0, ny - 1)]
    pltpu.make_async_copy(received, received, rows_sem.at[1]).wait()

    ring_docs = ny * train_docs

    def product(side):
        result = None
        for xl in range(2):
            queries = gathered[side, pl.ds(xl * groups, groups)].reshape(groups * tile_rows, lanes)
            documents = rows_all[pl.ds(side * (slab // 2) + xl * 2, 2)].reshape(2 * ring_docs, lanes)
            term = lax.dot_general(
                queries, documents, (((1,), (1,)), ((), ())), preferred_element_type=F32
            )
            result = term if result is None else result + term
        result = result.reshape(groups, 2, query_docs, 2 * ring_docs)
        return (result[:, 0, :, :ring_docs] + result[:, 1, :, ring_docs:]) * score_norm

    first = product(core)
    sib_copy.wait_recv()
    score_send[...] = first + product(1 - core)

    def send_scores(j, carry):
        other, target = score_partner(j)
        pltpu.make_async_remote_copy(
            src_ref=score_send.at[other],
            dst_ref=score_recv.at[query],
            send_sem=score_sem.at[0],
            recv_sem=score_sem.at[1],
            device_id=target,
            device_id_type=MESH,
        ).start()
        return carry

    lax.fori_loop(1, groups, send_scores, 0)
    score_recv[query] = score_send[query]

    sib_copy.wait_send()
    pltpu.make_async_copy(others, others, plane_sem.at[0]).wait()
    pltpu.make_async_copy(received, received, rows_sem.at[0]).wait()
    own_tile = y == z
    sent = pieces.at[pl.ds(0, nz * 2 - 1)]

    @pl.when(own_tile)
    def _():
        pltpu.make_async_copy(sent, sent, reduce_sem.at[0]).wait()

    @pl.when(jnp.logical_not(own_tile))
    def _():
        pltpu.make_async_copy(pieces, pieces, reduce_sem.at[0]).wait()

    blocks = score_recv.at[pl.ds(0, groups - 1)]
    pltpu.make_async_copy(blocks, blocks, score_sem.at[1]).wait()
    for side in range(2):
        value = score_recv[side * ny]
        for k in range(1, ny):
            value = value + score_recv[side * ny + k]
        out_ref[:, side * ring_docs:(side + 1) * ring_docs] = value
    pltpu.make_async_copy(blocks, blocks, score_sem.at[0]).wait()


def on_device(
    train_factors, train_lengths, query_factors, query_lengths, basis_out, basis_in, eigenvalues
):
    layer_count, rank, _ = basis_in.shape
    train_docs, _, slots, lanes = train_factors.shape
    query_docs = query_factors.shape[0]
    trains = lax.axis_size("train")
    groups = lax.axis_size("query")
    nz, ny = trains // 4, groups // 2
    slab = rank // ny
    tile_rows = 2 * query_docs
    batches = 2
    score_norm = 1.0 / (rank * math.sqrt(layer_count))
    train_norm = 1.0 / math.sqrt(slots)
    query_norm = 1.0 / math.sqrt(slots * trains)
    vmem = pl.BlockSpec(memory_space=pltpu.VMEM)
    hbm = pl.BlockSpec(memory_space=pltpu.HBM)
    dma = pltpu.SemaphoreType.DMA
    scores = pl.pallas_call(
        functools.partial(kernel, nz, ny, score_norm, train_norm, query_norm),
        out_shape=jax.ShapeDtypeStruct((query_docs, groups * train_docs), F32),
        in_specs=[hbm] * 7,
        out_specs=vmem,
        scratch_shapes=[
            pltpu.VMEM(train_factors.shape, BF16),
            pltpu.SMEM(train_lengths.shape, jnp.int32),
            pltpu.VMEM(query_factors.shape, BF16),
            pltpu.SMEM(query_lengths.shape, jnp.int32),
            pltpu.VMEM(basis_out.shape, F32),
            pltpu.VMEM(basis_in.shape, F32),
            pltpu.VMEM(eigenvalues.shape, F32),
            pltpu.VMEM((3 * lanes, lanes), BF16),
            pltpu.VMEM((lanes, 3 * rank), BF16),
            pltpu.VMEM((rank, lanes), F32),
            pltpu.VMEM((ny, 2, slab // 2, query_docs, lanes), F32),
            pltpu.VMEM((ny, slab // 2, query_docs, lanes), F32),
            pltpu.VMEM((nz * 2, 2, query_docs, lanes), F32),
            pltpu.VMEM((2, 2 * groups, tile_rows, lanes), BF16),
            pltpu.VMEM((rank, train_docs, lanes), F32),
            pltpu.VMEM((rank, batches, train_docs // batches, lanes), BF16),
            pltpu.VMEM((slab, ny, batches, train_docs // batches, lanes), BF16),
            pltpu.VMEM((groups, query_docs, ny * train_docs), F32),
            pltpu.VMEM((groups, query_docs, ny * train_docs), F32),
            dma((4,)),
            dma,
            dma((5,)),
            dma((2,)),
            dma((2,)),
            dma((2,)),
            dma((2,)),
            dma((2,)),
            dma((2,)),
        ],
        compiler_params=pltpu.CompilerParams(
            collective_id=0, has_side_effects=True, vmem_limit_bytes=64 * 1024 * 1024
        ),
        cost_estimate=pl.CostEstimate(flops=400_000_000, bytes_accessed=6_000_000, transcendentals=0),
    )(
        train_factors, train_lengths, query_factors, query_lengths, basis_out, basis_in, eigenvalues
    )
    return scores.T


def solution(mesh):
    return jax.shard_map(
        on_device,
        mesh=mesh,
        in_specs=(
            P(("train", "query"), None, None, None),
            P(("train", "query")),
            P("query", None, "train", None),
            P("query"),
            P(),
            P(),
            P(),
        ),
        out_specs=P("train", "query"),
        check_vma=False,
    )
```

```python
import functools
import math

import jax
import jax.numpy as jnp
from jax import lax
from jax.experimental import pallas as pl
from jax.experimental.pallas import tpu as pltpu
from jax.sharding import PartitionSpec as P

F32 = jnp.float32
BF16 = jnp.bfloat16
MESH = pl.DeviceIdType.MESH


def split(value):
    high = value.astype(BF16)
    return high, (value - high.astype(F32)).astype(BF16)


def mm(lhs, rhs):
    return jnp.dot(lhs, rhs, preferred_element_type=F32)


def kernel(
    nz, ny, score_norm, train_norm, query_norm,
    train_hbm, train_len_hbm, query_hbm, query_len_hbm, basis_out_hbm, basis_in_hbm, eigenvalues_hbm,
    out_ref,
    train_buf, train_len, query_buf, query_len, basis_out, basis_in, eigenvalues,
    right_ref, left_ref, scale_ref,
    partial, sibling_part, pieces, gathered, rotated, rows_own, rows_all, score_send, score_recv,
    load_sem, query_sem, small_sem, pair_sem, reduce_sem, plane_sem, sib_sem, rows_sem, score_sem,
):
    rank = basis_in.shape[1]
    lanes = 2 * rank
    train_docs = train_hbm.shape[0]
    query_docs = query_hbm.shape[0]
    slots = train_hbm.shape[2]
    slab = rank // ny
    groups = ny * 2
    plane = nz * 4
    tile_rows = 2 * query_docs

    train = lax.axis_index("train")
    query = lax.axis_index("query")
    z = train // 4
    x_lo = (train // 2) % 2
    core = train % 2
    x_hi = query // ny
    y = query % ny
    z_at = [lax.rem(z + k, nz) for k in range(nz)]
    y_at = [lax.rem(y + k, ny) for k in range(ny)]
    x_at = [(x_lo, x_hi), (1 - x_lo, x_hi), (x_lo, 1 - x_hi), (1 - x_lo, 1 - x_hi)]

    def hops(k, size):
        return min(k, size - k)

    plane_steps = [(k, m) for k in range(nz) for m in range(4) if k or m]
    plane_steps.sort(key=lambda step: -hops(step[0], nz) - (0, 1, 2, 1)[step[1]])
    score_steps = [(k, m) for k in range(ny) for m in range(2) if k or m]
    score_steps.sort(key=lambda step: -hops(step[0], ny) - 2 * step[1])
    ring_steps = sorted(range(1, ny), key=lambda k: -hops(k, ny))

    def device(dz, dxl, dxh, dy):
        return dz * 4 + dxl * 2 + core, dxh * ny + dy

    sibling = (train + 1 - 2 * core, query)

    def plane_partner(k, m):
        return device(z_at[k], x_at[m][0], x_at[m][1], y)

    def score_partner(k, m):
        dxh = 1 - x_hi if m else x_hi
        return dxh, y_at[k], (train, dxh * ny + y_at[k])

    load_query = pltpu.make_async_copy(query_hbm, query_buf, query_sem)
    load_query.start()
    small = [
        pltpu.make_async_copy(src, dst, small_sem.at[i])
        for i, (src, dst) in enumerate(
            [
                (query_len_hbm, query_len),
                (basis_in_hbm, basis_in),
                (basis_out_hbm, basis_out),
                (eigenvalues_hbm, eigenvalues),
                (train_len_hbm, train_len),
            ]
        )
    ]
    for copy in small:
        copy.start()
    parts = load_sem.shape[0]
    part_docs = train_docs // parts
    loads = []
    for i in range(parts):
        window = pl.ds(i * part_docs, part_docs)
        loads.append(pltpu.make_async_copy(train_hbm.at[window], train_buf.at[window], load_sem.at[i]))
        loads[-1].start()

    barrier = pltpu.get_barrier_semaphore()

    def greet(target):
        pl.semaphore_signal(barrier, inc=1, device_id=target, device_id_type=MESH)

    own_tile = y == z
    for k in range(nz):
        for half in range(2):
            source, group = device(z_at[k], half, x_hi, z)
            if k == 0:
                source = source + jnp.where(own_tile & (x_lo == half), 1 - 2 * core, 0)
            greet((source, group))
    for k, m in plane_steps:
        greet(plane_partner(k, m))
    for k, m in score_steps:
        greet(score_partner(k, m)[2])
    greet(sibling)
    greetings = 1 + nz * 2 + len(plane_steps) + len(score_steps)

    for copy in small:
        copy.wait()
    zero = jnp.zeros((rank, rank), F32)
    block = jnp.concatenate(
        [
            jnp.concatenate([basis_in[0], zero], axis=1),
            jnp.concatenate([zero, basis_in[1]], axis=1),
        ],
        axis=0,
    )
    high, low = split(block)
    right_ref[...] = jnp.concatenate([high, high, low], axis=0)
    turned = jnp.concatenate([basis_out[0].T, basis_out[1].T], axis=0)
    high, low = split(turned)
    left_ref[...] = jnp.concatenate([high, high, low], axis=1)
    scale_ref[...] = 1.0 / jnp.sqrt(jnp.concatenate([eigenvalues[0], eigenvalues[1]], axis=1))

    lane = lax.broadcasted_iota(jnp.int32, (rank, lanes), 1)
    first_layer = lane < rank
    token = lax.broadcasted_iota(jnp.int32, (slots, lanes), 0)

    def outer(factors, live):
        mask = jnp.where(token < live, 1.0, 0.0).astype(BF16)
        sums = []
        for layer in range(2):
            tokens = factors[layer]
            masked = tokens * mask
            product = lax.dot_general(
                masked, tokens, (((0,), (0,)), ((), ())), preferred_element_type=F32
            )
            sums.append(product[rank:])
        return jnp.where(first_layer, sums[0], pltpu.roll(sums[1], rank, 1))

    def rotate(summed, norm):
        count = len(summed)
        high, low = split(jnp.concatenate(summed, axis=0))
        turned = mm(jnp.concatenate([high, low, high], axis=1), right_ref[...])
        high, low = split(turned)
        columns = []
        for i in range(count):
            rows = slice(i * rank, (i + 1) * rank)
            columns.append(jnp.concatenate([high[rows], low[rows], high[rows]], axis=0))
        product = mm(left_ref[...], jnp.concatenate(columns, axis=1))
        scale = scale_ref[...] * norm
        results = []
        for i in range(count):
            mine = product[:, i * lanes:(i + 1) * lanes]
            results.append(jnp.where(first_layer, mine[:rank], mine[rank:]) * scale)
        return results

    load_query.wait()
    query_batch = 4

    def query_step(step, carry):
        summed = []
        for i in range(query_batch):
            doc = step * query_batch + i
            summed.append(outer(query_buf[doc], query_len[doc] - train * slots))
        for i, value in enumerate(rotate(summed, query_norm)):
            partial[:, :, :, pl.ds(step * query_batch + i, 1), :] = value.reshape(ny, 2, slab // 2, 1, lanes)
        return carry

    lax.fori_loop(0, query_docs // query_batch, query_step, 0)

    pl.semaphore_wait(barrier, greetings)
    pair_copy = pltpu.make_async_remote_copy(
        src_ref=partial.at[:, 1 - core],
        dst_ref=sibling_part,
        send_sem=pair_sem.at[0],
        recv_sem=pair_sem.at[1],
        device_id=sibling,
        device_id_type=MESH,
    )
    pair_copy.start()

    train_batch = 4
    per_part = part_docs // train_batch

    def train_step(step, carry):
        summed = []
        for i in range(train_batch):
            doc = step * train_batch + i
            summed.append(outer(train_buf[doc], train_len[doc]))
        for i, value in enumerate(rotate(summed, train_norm)):
            rotated[:, pl.ds(step * train_batch + i, 1), :] = value[:, None, :]
        return carry

    def train_part(i):
        loads[i].wait()
        lax.fori_loop(i * per_part, (i + 1) * per_part, train_step, 0)

    batches = rows_own.shape[1]
    batch_docs = train_docs // batches

    def send_rows(i):
        rows_own[:, i] = rotated[:, i * batch_docs:(i + 1) * batch_docs, :].astype(BF16)

        for k in ring_steps:
            pltpu.make_async_remote_copy(
                src_ref=rows_own.at[pl.ds(y_at[k] * slab, slab), i],
                dst_ref=rows_all.at[:, y, i],
                send_sem=rows_sem.at[0],
                recv_sem=rows_sem.at[1],
                device_id=device(z, x_lo, x_hi, y_at[k]),
                device_id_type=MESH,
            ).start()
        rows_all[:, y, i] = rows_own[pl.ds(y * slab, slab), i]

    pair_copy.wait()
    sibling_part[...] = sibling_part[...] + partial[:, core]

    def send_reduce(s, half, target):
        pltpu.make_async_remote_copy(
            src_ref=sibling_part.at[s, pl.ds(half * 2, 2)],
            dst_ref=pieces.at[z * 2 + x_lo],
            send_sem=reduce_sem.at[0],
            recv_sem=reduce_sem.at[1],
            device_id=target,
            device_id_type=MESH,
        ).start()

    for k in ring_steps:
        for half in range(2):
            send_reduce(y_at[k], half, device(y, half, x_hi, y_at[k]))
    for half in range(2):
        itself = own_tile & (x_lo == half)

        @pl.when(itself)
        def _(half=half):
            src, dst = sibling_part.at[y, pl.ds(half * 2, 2)], pieces.at[z * 2 + x_lo]
            pltpu.make_async_copy(src, dst, reduce_sem.at[1]).start()

        @pl.when(jnp.logical_not(itself))
        def _(half=half):
            send_reduce(y, half, device(y, half, x_hi, y))

    train_part(0)
    train_part(1)
    send_rows(0)
    train_part(2)
    train_part(3)
    send_rows(1)
    pltpu.make_async_copy(pieces, pieces, reduce_sem.at[1]).wait()
    total = pieces[0]
    for j in range(1, nz * 2):
        total = total + pieces[j]
    gathered[core, z * 4 + x_lo * 2 + x_hi] = total.reshape(tile_rows, lanes).astype(BF16)

    mine = gathered.at[core, z * 4 + x_lo * 2 + x_hi]
    near = [k for k in range(nz) if hops(k, nz) <= 2]
    far = [k for k in range(nz) if hops(k, nz) > 2]
    for k, m in plane_steps:
        sems = plane_sem.at[1 if k in near else 2]
        pltpu.make_async_remote_copy(
            src_ref=mine,
            dst_ref=mine,
            send_sem=plane_sem.at[0],
            recv_sem=sems,
            device_id=plane_partner(k, m),
            device_id_type=MESH,
        ).start()

    def forward(k):
        window = gathered.at[core, pl.ds(z_at[k] * 4, 4)]
        pltpu.make_async_remote_copy(
            src_ref=window,
            dst_ref=window,
            send_sem=sib_sem.at[0],
            recv_sem=sib_sem.at[1],
            device_id=sibling,
            device_id_type=MESH,
        ).start()

    arrived = gathered.at[0, pl.ds(0, len(near) * 4 - 1)]
    pltpu.make_async_copy(arrived, arrived, plane_sem.at[1]).wait()
    for k in near:
        forward(k)
    if far:
        arrived = gathered.at[0, pl.ds(0, len(far) * 4)]
        pltpu.make_async_copy(arrived, arrived, plane_sem.at[2]).wait()
        for k in far:
            forward(k)
    received = rows_all.at[:, pl.ds(0, ny - 1)]
    pltpu.make_async_copy(received, received, rows_sem.at[1]).wait()

    ring_docs = ny * train_docs

    def product(side):
        result = None
        for xl in range(2):
            queries = jnp.concatenate(
                [gathered[side, i * 4 + xl * 2 + xh] for i in range(nz) for xh in range(2)], axis=0
            )
            documents = rows_all[pl.ds(side * (slab // 2) + xl * 2, 2)].reshape(2 * ring_docs, lanes)
            term = lax.dot_general(
                queries, documents, (((1,), (1,)), ((), ())), preferred_element_type=F32
            )
            result = term if result is None else result + term
        result = result.reshape(groups, 2, query_docs, 2 * ring_docs)
        return (result[:, 0, :, :ring_docs] + result[:, 1, :, ring_docs:]) * score_norm

    first = product(core)
    half_tiles = gathered.at[0]
    pltpu.make_async_copy(half_tiles, half_tiles, sib_sem.at[1]).wait()
    score_send[...] = first + product(1 - core)

    for k, m in score_steps:
        dxh, dy, target = score_partner(k, m)
        pltpu.make_async_remote_copy(
            src_ref=score_send.at[dy * 2 + dxh],
            dst_ref=score_recv.at[query],
            send_sem=score_sem.at[0],
            recv_sem=score_sem.at[1],
            device_id=target,
            device_id_type=MESH,
        ).start()
    score_recv[query] = score_send[y * 2 + x_hi]

    pltpu.make_async_copy(half_tiles, half_tiles, sib_sem.at[0]).wait()
    others = gathered.at[0, pl.ds(0, len(plane_steps))]
    pltpu.make_async_copy(others, others, plane_sem.at[0]).wait()
    pltpu.make_async_copy(received, received, rows_sem.at[0]).wait()
    sent = pieces.at[pl.ds(0, nz * 2 - 1)]

    @pl.when(own_tile)
    def _():
        pltpu.make_async_copy(sent, sent, reduce_sem.at[0]).wait()

    @pl.when(jnp.logical_not(own_tile))
    def _():
        pltpu.make_async_copy(pieces, pieces, reduce_sem.at[0]).wait()

    blocks = score_recv.at[pl.ds(0, groups - 1)]
    pltpu.make_async_copy(blocks, blocks, score_sem.at[1]).wait()
    for side in range(2):
        value = score_recv[side * ny]
        for k in range(1, ny):
            value = value + score_recv[side * ny + k]
        out_ref[:, side * ring_docs:(side + 1) * ring_docs] = value
    pltpu.make_async_copy(blocks, blocks, score_sem.at[0]).wait()


def on_device(
    train_factors, train_lengths, query_factors, query_lengths, basis_out, basis_in, eigenvalues
):
    layer_count, rank, _ = basis_in.shape
    train_docs, _, slots, lanes = train_factors.shape
    query_docs = query_factors.shape[0]
    trains = lax.axis_size("train")
    groups = lax.axis_size("query")
    nz, ny = trains // 4, groups // 2
    slab = rank // ny
    tile_rows = 2 * query_docs
    batches = 2
    score_norm = 1.0 / (rank * math.sqrt(layer_count))
    train_norm = 1.0 / math.sqrt(slots)
    query_norm = 1.0 / math.sqrt(slots * trains)
    vmem = pl.BlockSpec(memory_space=pltpu.VMEM)
    hbm = pl.BlockSpec(memory_space=pltpu.HBM)
    dma = pltpu.SemaphoreType.DMA
    scores = pl.pallas_call(
        functools.partial(kernel, nz, ny, score_norm, train_norm, query_norm),
        out_shape=jax.ShapeDtypeStruct((query_docs, groups * train_docs), F32),
        in_specs=[hbm] * 7,
        out_specs=vmem,
        scratch_shapes=[
            pltpu.VMEM(train_factors.shape, BF16),
            pltpu.SMEM(train_lengths.shape, jnp.int32),
            pltpu.VMEM(query_factors.shape, BF16),
            pltpu.SMEM(query_lengths.shape, jnp.int32),
            pltpu.VMEM(basis_out.shape, F32),
            pltpu.VMEM(basis_in.shape, F32),
            pltpu.VMEM(eigenvalues.shape, F32),
            pltpu.VMEM((3 * lanes, lanes), BF16),
            pltpu.VMEM((lanes, 3 * rank), BF16),
            pltpu.VMEM((rank, lanes), F32),
            pltpu.VMEM((ny, 2, slab // 2, query_docs, lanes), F32),
            pltpu.VMEM((ny, slab // 2, query_docs, lanes), F32),
            pltpu.VMEM((nz * 2, 2, query_docs, lanes), F32),
            pltpu.VMEM((2, nz * 4, tile_rows, lanes), BF16),
            pltpu.VMEM((rank, train_docs, lanes), F32),
            pltpu.VMEM((rank, batches, train_docs // batches, lanes), BF16),
            pltpu.VMEM((slab, ny, batches, train_docs // batches, lanes), BF16),
            pltpu.VMEM((groups, query_docs, ny * train_docs), F32),
            pltpu.VMEM((groups, query_docs, ny * train_docs), F32),
            dma((4,)),
            dma,
            dma((5,)),
            dma((2,)),
            dma((2,)),
            dma((3,)),
            dma((2,)),
            dma((2,)),
            dma((2,)),
        ],
        compiler_params=pltpu.CompilerParams(
            collective_id=0, has_side_effects=True, vmem_limit_bytes=64 * 1024 * 1024
        ),
        cost_estimate=pl.CostEstimate(flops=400_000_000, bytes_accessed=6_000_000, transcendentals=0),
    )(
        train_factors, train_lengths, query_factors, query_lengths, basis_out, basis_in, eigenvalues
    )
    return scores.T


def solution(mesh):
    return jax.shard_map(
        on_device,
        mesh=mesh,
        in_specs=(
            P(("train", "query"), None, None, None),
            P(("train", "query")),
            P("query", None, "train", None),
            P("query"),
            P(),
            P(),
            P(),
        ),
        out_specs=P("train", "query"),
        check_vma=False,
    )
```

```python
import functools
import math

import jax
import jax.numpy as jnp
from jax import lax
from jax.experimental import pallas as pl
from jax.experimental.pallas import tpu as pltpu
from jax.sharding import PartitionSpec as P

F32 = jnp.float32
BF16 = jnp.bfloat16
MESH = pl.DeviceIdType.MESH


def split(value):
    high = value.astype(BF16)
    return high, (value - high.astype(F32)).astype(BF16)


def mm(lhs, rhs):
    return jnp.dot(lhs, rhs, preferred_element_type=F32)


def kernel(
    nz, ny, score_norm, train_norm, query_norm,
    train_hbm, train_len_hbm, query_hbm, query_len_hbm, basis_out_hbm, basis_in_hbm, eigenvalues_hbm,
    out_ref,
    train_buf, train_len, query_buf, query_len, basis_out, basis_in, eigenvalues,
    right_ref, left_ref, scale_ref,
    partial, sibling_part, sums_ref, pieces, gathered, rotated, rows_own, rows_all, score_send, score_recv,
    load_sem, query_sem, small_sem, pair_sem, reduce_sem, plane_sem, sib_sem, rows_sem, score_sem,
):
    rank = basis_in.shape[1]
    lanes = 2 * rank
    train_docs = train_hbm.shape[0]
    query_docs = query_hbm.shape[0]
    slots = train_hbm.shape[2]
    slab = rank // ny
    groups = ny * 2
    plane = nz * 4
    tile_rows = 2 * query_docs

    train = lax.axis_index("train")
    query = lax.axis_index("query")
    z = train // 4
    x_lo = (train // 2) % 2
    core = train % 2
    x_hi = query // ny
    y = query % ny
    z_at = [lax.rem(z + k, nz) for k in range(nz)]
    y_at = [lax.rem(y + k, ny) for k in range(ny)]
    x_at = [(x_lo, x_hi), (1 - x_lo, x_hi), (x_lo, 1 - x_hi), (1 - x_lo, 1 - x_hi)]

    def hops(k, size):
        return min(k, size - k)

    plane_steps = [(k, m) for k in range(nz) for m in range(4) if k or m]
    plane_steps.sort(key=lambda step: -hops(step[0], nz) - (0, 1, 2, 1)[step[1]])
    score_steps = [(k, m) for k in range(ny) for m in range(2) if k or m]
    score_steps.sort(key=lambda step: -hops(step[0], ny) - 2 * step[1])
    ring_steps = sorted(range(1, ny), key=lambda k: -hops(k, ny))

    def device(dz, dxl, dxh, dy):
        return dz * 4 + dxl * 2 + core, dxh * ny + dy

    sibling = (train + 1 - 2 * core, query)

    def plane_partner(k, m):
        return device(z_at[k], x_at[m][0], x_at[m][1], y)

    def score_partner(k, m):
        dxh = 1 - x_hi if m else x_hi
        return dxh, y_at[k], (train, dxh * ny + y_at[k])

    load_query = pltpu.make_async_copy(query_hbm, query_buf, query_sem)
    load_query.start()
    barrier = pltpu.get_barrier_semaphore()

    def greet(target):
        pl.semaphore_signal(barrier, inc=1, device_id=target, device_id_type=MESH)

    own_tile = y == z
    for k in sorted(range(nz), key=lambda k: -hops(k, nz)):
        for half in range(2):
            source, group = device(z_at[k], half, x_hi, z)
            if k == 0:
                source = source + jnp.where(own_tile & (x_lo == half), 1 - 2 * core, 0)
            greet((source, group))
    for k, m in score_steps:
        greet(score_partner(k, m)[2])
    for k, m in plane_steps:
        greet(plane_partner(k, m))
    greet(sibling)
    greetings = 1 + nz * 2 + len(plane_steps) + len(score_steps)

    small = [
        pltpu.make_async_copy(src, dst, small_sem.at[i])
        for i, (src, dst) in enumerate(
            [
                (query_len_hbm, query_len),
                (basis_in_hbm, basis_in),
                (basis_out_hbm, basis_out),
                (eigenvalues_hbm, eigenvalues),
                (train_len_hbm, train_len),
            ]
        )
    ]
    for copy in small:
        copy.start()
    parts = load_sem.shape[0]
    part_docs = train_docs // parts
    loads = []
    for i in range(parts):
        window = pl.ds(i * part_docs, part_docs)
        loads.append(pltpu.make_async_copy(train_hbm.at[window], train_buf.at[window], load_sem.at[i]))
        loads[-1].start()

    for copy in small:
        copy.wait()
    zero = jnp.zeros((rank, rank), F32)
    block = jnp.concatenate(
        [
            jnp.concatenate([basis_in[0], zero], axis=1),
            jnp.concatenate([zero, basis_in[1]], axis=1),
        ],
        axis=0,
    )
    high, low = split(block)
    right_ref[...] = jnp.concatenate([high, high, low], axis=0)
    turned = jnp.concatenate([basis_out[0].T, basis_out[1].T], axis=0)
    high, low = split(turned)
    left_ref[...] = jnp.concatenate([high, high, low], axis=1)
    scale_ref[...] = 1.0 / jnp.sqrt(jnp.concatenate([eigenvalues[0], eigenvalues[1]], axis=1))

    lane = lax.broadcasted_iota(jnp.int32, (rank, lanes), 1)
    first_layer = lane < rank
    token = lax.broadcasted_iota(jnp.int32, (slots, lanes), 0)

    def outer(factors, live):
        mask = jnp.where(token < live, 1.0, 0.0).astype(BF16)
        sums = []
        for layer in range(2):
            tokens = factors[layer]
            masked = tokens * mask
            product = lax.dot_general(
                masked, tokens, (((0,), (0,)), ((), ())), preferred_element_type=F32
            )
            sums.append(product[rank:])
        return jnp.where(first_layer, sums[0], pltpu.roll(sums[1], rank, 1))

    def rotate(summed, norm):
        count = len(summed)
        high, low = split(jnp.concatenate(summed, axis=0))
        turned = mm(jnp.concatenate([high, low, high], axis=1), right_ref[...])
        high, low = split(turned)
        columns = []
        for i in range(count):
            rows = slice(i * rank, (i + 1) * rank)
            columns.append(jnp.concatenate([high[rows], low[rows], high[rows]], axis=0))
        product = mm(left_ref[...], jnp.concatenate(columns, axis=1))
        scale = scale_ref[...] * norm
        results = []
        for i in range(count):
            mine = product[:, i * lanes:(i + 1) * lanes]
            results.append(jnp.where(first_layer, mine[:rank], mine[rank:]) * scale)
        return results

    load_query.wait()
    query_batch = 4

    def query_step(step, carry):
        summed = []
        for i in range(query_batch):
            doc = step * query_batch + i
            summed.append(outer(query_buf[doc], query_len[doc] - train * slots))
        for i, value in enumerate(rotate(summed, query_norm)):
            partial[:, :, :, pl.ds(step * query_batch + i, 1), :] = value.reshape(ny, 2, slab // 2, 1, lanes)
        return carry

    lax.fori_loop(0, query_docs // query_batch, query_step, 0)

    pl.semaphore_wait(barrier, greetings)
    pair_copy = pltpu.make_async_remote_copy(
        src_ref=partial.at[:, 1 - core],
        dst_ref=sibling_part,
        send_sem=pair_sem.at[0],
        recv_sem=pair_sem.at[1],
        device_id=sibling,
        device_id_type=MESH,
    )
    pair_copy.start()

    train_batch = 4
    per_part = part_docs // train_batch

    def train_step(step, carry):
        summed = []
        for i in range(train_batch):
            doc = step * train_batch + i
            summed.append(outer(train_buf[doc], train_len[doc]))
        for i, value in enumerate(rotate(summed, train_norm)):
            rotated[:, pl.ds(step * train_batch + i, 1), :] = value[:, None, :]
        return carry

    def train_part(i):
        loads[i].wait()
        lax.fori_loop(i * per_part, (i + 1) * per_part, train_step, 0)

    batches = rows_own.shape[1]
    batch_docs = train_docs // batches

    def send_rows(i):
        rows_own[:, i] = rotated[:, i * batch_docs:(i + 1) * batch_docs, :].astype(BF16)

        for k in ring_steps:
            pltpu.make_async_remote_copy(
                src_ref=rows_own.at[pl.ds(y_at[k] * slab, slab), i],
                dst_ref=rows_all.at[:, y, i],
                send_sem=rows_sem.at[0],
                recv_sem=rows_sem.at[1],
                device_id=device(z, x_lo, x_hi, y_at[k]),
                device_id_type=MESH,
            ).start()
        rows_all[:, y, i] = rows_own[pl.ds(y * slab, slab), i]

    train_part(0)
    pair_copy.wait()
    sums = sibling_part[...] + partial[:, core]
    sums_ref[...] = sums.reshape(ny, 2, tile_rows, lanes).astype(BF16)

    def send_reduce(s, half, target):
        pltpu.make_async_remote_copy(
            src_ref=sums_ref.at[s, half],
            dst_ref=pieces.at[z * 2 + x_lo],
            send_sem=reduce_sem.at[0],
            recv_sem=reduce_sem.at[1],
            device_id=target,
            device_id_type=MESH,
        ).start()

    for k in ring_steps:
        for half in range(2):
            send_reduce(y_at[k], half, device(y, half, x_hi, y_at[k]))
    for half in range(2):
        itself = own_tile & (x_lo == half)

        @pl.when(itself)
        def _(half=half):
            src, dst = sums_ref.at[y, half], pieces.at[z * 2 + x_lo]
            pltpu.make_async_copy(src, dst, reduce_sem.at[1]).start()

        @pl.when(jnp.logical_not(itself))
        def _(half=half):
            send_reduce(y, half, device(y, half, x_hi, y))

    train_part(1)
    send_rows(0)
    train_part(2)
    train_part(3)
    send_rows(1)
    pltpu.make_async_copy(pieces, pieces, reduce_sem.at[1]).wait()
    total = pieces[0].astype(F32)
    for j in range(1, nz * 2):
        total = total + pieces[j].astype(F32)
    gathered[core, z * 4 + x_lo * 2 + x_hi] = total.astype(BF16)

    mine = gathered.at[core, z * 4 + x_lo * 2 + x_hi]
    distances = nz // 2 + 1
    for k, m in plane_steps:
        pltpu.make_async_remote_copy(
            src_ref=mine,
            dst_ref=mine,
            send_sem=plane_sem.at[0],
            recv_sem=plane_sem.at[1 + hops(k, nz)],
            device_id=plane_partner(k, m),
            device_id_type=MESH,
        ).start()

    def forward(k):
        window = gathered.at[core, pl.ds(z_at[k] * 4, 4)]
        pltpu.make_async_remote_copy(
            src_ref=window,
            dst_ref=window,
            send_sem=sib_sem.at[0],
            recv_sem=sib_sem.at[1],
            device_id=sibling,
            device_id_type=MESH,
        ).start()

    for distance in range(distances):
        places = [k for k in range(nz) if hops(k, nz) == distance]
        arrived = gathered.at[0, pl.ds(0, len(places) * 4 - (distance == 0))]
        pltpu.make_async_copy(arrived, arrived, plane_sem.at[1 + distance]).wait()
        for k in places:
            forward(k)
    received = rows_all.at[:, pl.ds(0, ny - 1)]
    pltpu.make_async_copy(received, received, rows_sem.at[1]).wait()

    ring_docs = ny * train_docs

    def product(side):
        result = None
        for xl in range(2):
            queries = jnp.concatenate(
                [gathered[side, i * 4 + xl * 2 + xh] for i in range(nz) for xh in range(2)], axis=0
            )
            documents = rows_all[pl.ds(side * (slab // 2) + xl * 2, 2)].reshape(2 * ring_docs, lanes)
            term = lax.dot_general(
                queries, documents, (((1,), (1,)), ((), ())), preferred_element_type=F32
            )
            result = term if result is None else result + term
        result = result.reshape(groups, 2, query_docs, 2 * ring_docs)
        return (result[:, 0, :, :ring_docs] + result[:, 1, :, ring_docs:]) * score_norm

    first = product(core)
    half_tiles = gathered.at[0]
    pltpu.make_async_copy(half_tiles, half_tiles, sib_sem.at[1]).wait()
    scores = first + product(1 - core)
    width = ring_docs // 2
    score_send[...] = jnp.concatenate([scores[:, :, :width], scores[:, :, width:]], axis=1).astype(BF16)

    for k, m in score_steps:
        dxh, dy, target = score_partner(k, m)
        pltpu.make_async_remote_copy(
            src_ref=score_send.at[dy * 2 + dxh],
            dst_ref=score_recv.at[query],
            send_sem=score_sem.at[0],
            recv_sem=score_sem.at[1],
            device_id=target,
            device_id_type=MESH,
        ).start()
    score_recv[query] = score_send[y * 2 + x_hi]

    pltpu.make_async_copy(half_tiles, half_tiles, sib_sem.at[0]).wait()
    others = gathered.at[0, pl.ds(0, len(plane_steps))]
    pltpu.make_async_copy(others, others, plane_sem.at[0]).wait()
    pltpu.make_async_copy(received, received, rows_sem.at[0]).wait()
    sent = pieces.at[pl.ds(0, nz * 2 - 1)]

    @pl.when(own_tile)
    def _():
        pltpu.make_async_copy(sent, sent, reduce_sem.at[0]).wait()

    @pl.when(jnp.logical_not(own_tile))
    def _():
        pltpu.make_async_copy(pieces, pieces, reduce_sem.at[0]).wait()

    blocks = score_recv.at[pl.ds(0, groups - 1)]
    pltpu.make_async_copy(blocks, blocks, score_sem.at[1]).wait()
    for side in range(2):
        value = score_recv[side * ny].astype(F32)
        for k in range(1, ny):
            value = value + score_recv[side * ny + k].astype(F32)
        out_ref[:, side * ring_docs:side * ring_docs + width] = value[:query_docs]
        out_ref[:, side * ring_docs + width:(side + 1) * ring_docs] = value[query_docs:]
    pltpu.make_async_copy(blocks, blocks, score_sem.at[0]).wait()


def on_device(
    train_factors, train_lengths, query_factors, query_lengths, basis_out, basis_in, eigenvalues
):
    layer_count, rank, _ = basis_in.shape
    train_docs, _, slots, lanes = train_factors.shape
    query_docs = query_factors.shape[0]
    trains = lax.axis_size("train")
    groups = lax.axis_size("query")
    nz, ny = trains // 4, groups // 2
    slab = rank // ny
    tile_rows = 2 * query_docs
    batches = 2
    score_norm = 1.0 / (rank * math.sqrt(layer_count))
    train_norm = 1.0 / math.sqrt(slots)
    query_norm = 1.0 / math.sqrt(slots * trains)
    vmem = pl.BlockSpec(memory_space=pltpu.VMEM)
    hbm = pl.BlockSpec(memory_space=pltpu.HBM)
    dma = pltpu.SemaphoreType.DMA
    scores = pl.pallas_call(
        functools.partial(kernel, nz, ny, score_norm, train_norm, query_norm),
        out_shape=jax.ShapeDtypeStruct((query_docs, groups * train_docs), F32),
        in_specs=[hbm] * 7,
        out_specs=vmem,
        scratch_shapes=[
            pltpu.VMEM(train_factors.shape, BF16),
            pltpu.SMEM(train_lengths.shape, jnp.int32),
            pltpu.VMEM(query_factors.shape, BF16),
            pltpu.SMEM(query_lengths.shape, jnp.int32),
            pltpu.VMEM(basis_out.shape, F32),
            pltpu.VMEM(basis_in.shape, F32),
            pltpu.VMEM(eigenvalues.shape, F32),
            pltpu.VMEM((3 * lanes, lanes), BF16),
            pltpu.VMEM((lanes, 3 * rank), BF16),
            pltpu.VMEM((rank, lanes), F32),
            pltpu.VMEM((ny, 2, slab // 2, query_docs, lanes), F32),
            pltpu.VMEM((ny, slab // 2, query_docs, lanes), F32),
            pltpu.VMEM((ny, 2, tile_rows, lanes), BF16),
            pltpu.VMEM((nz * 2, tile_rows, lanes), BF16),
            pltpu.VMEM((2, nz * 4, tile_rows, lanes), BF16),
            pltpu.VMEM((rank, train_docs, lanes), F32),
            pltpu.VMEM((rank, batches, train_docs // batches, lanes), BF16),
            pltpu.VMEM((slab, ny, batches, train_docs // batches, lanes), BF16),
            pltpu.VMEM((groups, tile_rows, ny * train_docs // 2), BF16),
            pltpu.VMEM((groups, tile_rows, ny * train_docs // 2), BF16),
            dma((4,)),
            dma,
            dma((5,)),
            dma((2,)),
            dma((2,)),
            dma((nz // 2 + 2,)),
            dma((2,)),
            dma((2,)),
            dma((2,)),
        ],
        compiler_params=pltpu.CompilerParams(
            collective_id=0, has_side_effects=True, vmem_limit_bytes=64 * 1024 * 1024
        ),
        cost_estimate=pl.CostEstimate(flops=400_000_000, bytes_accessed=6_000_000, transcendentals=0),
    )(
        train_factors, train_lengths, query_factors, query_lengths, basis_out, basis_in, eigenvalues
    )
    return scores.T


def solution(mesh):
    return jax.shard_map(
        on_device,
        mesh=mesh,
        in_specs=(
            P(("train", "query"), None, None, None),
            P(("train", "query")),
            P("query", None, "train", None),
            P("query"),
            P(),
            P(),
            P(),
        ),
        out_specs=P("train", "query"),
        check_vma=False,
    )
```

```python
import functools
import math

import jax
import jax.numpy as jnp
from jax import lax
from jax.experimental import pallas as pl
from jax.experimental.pallas import tpu as pltpu
from jax.sharding import PartitionSpec as P

F32 = jnp.float32
BF16 = jnp.bfloat16
MESH = pl.DeviceIdType.MESH


def split(value):
    high = value.astype(BF16)
    return high, (value - high.astype(F32)).astype(BF16)


def mm(lhs, rhs):
    return jnp.dot(lhs, rhs, preferred_element_type=F32)


def kernel(
    nz, ny, score_norm, train_norm, query_norm,
    train_hbm, train_len_hbm, query_hbm, query_len_hbm, basis_out_hbm, basis_in_hbm, eigenvalues_hbm,
    out_ref,
    train_buf, train_len, query_buf, query_len, basis_out, basis_in, eigenvalues,
    right_ref, left_ref, scale_ref,
    partial, sibling_part, sums_ref, pieces, gathered, rotated, rows_own, rows_all, score_send, score_recv,
    load_sem, query_sem, small_sem, pair_sem, reduce_sem, plane_sem, sib_sem, rows_sem, score_sem,
):
    rank = basis_in.shape[1]
    lanes = 2 * rank
    train_docs = train_hbm.shape[0]
    query_docs = query_hbm.shape[0]
    slots = train_hbm.shape[2]
    slab = rank // ny
    groups = ny * 2
    plane = nz * 4
    tile_rows = 2 * query_docs

    train = lax.axis_index("train")
    query = lax.axis_index("query")
    z = train // 4
    x_lo = (train // 2) % 2
    core = train % 2
    x_hi = query // ny
    y = query % ny
    z_at = [lax.rem(z + k, nz) for k in range(nz)]
    y_at = [lax.rem(y + k, ny) for k in range(ny)]
    x_at = [(x_lo, x_hi), (1 - x_lo, x_hi), (x_lo, 1 - x_hi), (1 - x_lo, 1 - x_hi)]

    def hops(k, size):
        return min(k, size - k)

    plane_steps = [(k, m) for k in range(nz) for m in range(4) if k or m]
    plane_steps.sort(key=lambda step: -hops(step[0], nz) - (0, 1, 2, 1)[step[1]])
    score_steps = [(k, m) for k in range(ny) for m in range(2) if k or m]
    score_steps.sort(key=lambda step: -hops(step[0], ny) - 2 * step[1])
    ring_steps = sorted(range(1, ny), key=lambda k: -hops(k, ny))

    def device(dz, dxl, dxh, dy):
        return dz * 4 + dxl * 2 + core, dxh * ny + dy

    sibling = (train + 1 - 2 * core, query)

    def plane_partner(k, m):
        return device(z_at[k], x_at[m][0], x_at[m][1], y)

    def score_partner(k, m):
        dxh = 1 - x_hi if m else x_hi
        return dxh, y_at[k], (train, dxh * ny + y_at[k])

    load_query = pltpu.make_async_copy(query_hbm, query_buf, query_sem)
    load_query.start()
    small = [
        pltpu.make_async_copy(src, dst, small_sem.at[i])
        for i, (src, dst) in enumerate(
            [
                (query_len_hbm, query_len),
                (basis_in_hbm, basis_in),
                (basis_out_hbm, basis_out),
                (eigenvalues_hbm, eigenvalues),
                (train_len_hbm, train_len),
            ]
        )
    ]
    for copy in small:
        copy.start()
    barrier = pltpu.get_barrier_semaphore()

    def greet(target):
        pl.semaphore_signal(barrier, inc=1, device_id=target, device_id_type=MESH)

    own_tile = y == z
    for k in sorted(range(nz), key=lambda k: -hops(k, nz)):
        for half in range(2):
            source, group = device(z_at[k], half, x_hi, z)
            if k == 0:
                source = source + jnp.where(own_tile & (x_lo == half), 1 - 2 * core, 0)
            greet((source, group))
    for k, m in score_steps:
        greet(score_partner(k, m)[2])
    for k, m in plane_steps:
        greet(plane_partner(k, m))
    greet(sibling)
    greetings = 1 + nz * 2 + len(plane_steps) + len(score_steps)

    parts = load_sem.shape[0]
    part_docs = train_docs // parts
    loads = []
    for i in range(parts):
        window = pl.ds(i * part_docs, part_docs)
        loads.append(pltpu.make_async_copy(train_hbm.at[window], train_buf.at[window], load_sem.at[i]))
        loads[-1].start()

    for copy in small:
        copy.wait()
    zero = jnp.zeros((rank, rank), F32)
    block = jnp.concatenate(
        [
            jnp.concatenate([basis_in[0], zero], axis=1),
            jnp.concatenate([zero, basis_in[1]], axis=1),
        ],
        axis=0,
    )
    high, low = split(block)
    right_ref[...] = jnp.concatenate([high, high, low], axis=0)
    turned = jnp.concatenate([basis_out[0].T, basis_out[1].T], axis=0)
    high, low = split(turned)
    left_ref[...] = jnp.concatenate([high, high, low], axis=1)
    scale_ref[...] = 1.0 / jnp.sqrt(jnp.concatenate([eigenvalues[0], eigenvalues[1]], axis=1))

    lane = lax.broadcasted_iota(jnp.int32, (rank, lanes), 1)
    first_layer = lane < rank
    token = lax.broadcasted_iota(jnp.int32, (slots, lanes), 0)

    def outer(factors, live):
        mask = jnp.where(token < live, 1.0, 0.0).astype(BF16)
        sums = []
        for layer in range(2):
            tokens = factors[layer]
            masked = tokens * mask
            product = lax.dot_general(
                masked, tokens, (((0,), (0,)), ((), ())), preferred_element_type=F32
            )
            sums.append(product[rank:])
        return jnp.where(first_layer, sums[0], pltpu.roll(sums[1], rank, 1))

    def rotate(summed, norm):
        count = len(summed)
        high, low = split(jnp.concatenate(summed, axis=0))
        turned = mm(jnp.concatenate([high, low, high], axis=1), right_ref[...])
        high, low = split(turned)
        columns = []
        for i in range(count):
            rows = slice(i * rank, (i + 1) * rank)
            columns.append(jnp.concatenate([high[rows], low[rows], high[rows]], axis=0))
        product = mm(left_ref[...], jnp.concatenate(columns, axis=1))
        scale = scale_ref[...] * norm
        results = []
        for i in range(count):
            mine = product[:, i * lanes:(i + 1) * lanes]
            results.append(jnp.where(first_layer, mine[:rank], mine[rank:]) * scale)
        return results

    load_query.wait()
    query_batch = 8

    def query_step(step, carry):
        summed = []
        for i in range(query_batch):
            doc = step * query_batch + i
            summed.append(outer(query_buf[doc], query_len[doc] - train * slots))
        for i, value in enumerate(rotate(summed, query_norm)):
            partial[:, :, :, pl.ds(step * query_batch + i, 1), :] = value.reshape(ny, 2, slab // 2, 1, lanes)
        return carry

    lax.fori_loop(0, query_docs // query_batch, query_step, 0)

    pl.semaphore_wait(barrier, greetings)
    pair_copy = pltpu.make_async_remote_copy(
        src_ref=partial.at[:, 1 - core],
        dst_ref=sibling_part,
        send_sem=pair_sem.at[0],
        recv_sem=pair_sem.at[1],
        device_id=sibling,
        device_id_type=MESH,
    )
    pair_copy.start()

    train_batch = 4
    per_part = part_docs // train_batch

    def train_step(step, carry):
        summed = []
        for i in range(train_batch):
            doc = step * train_batch + i
            summed.append(outer(train_buf[doc], train_len[doc]))
        for i, value in enumerate(rotate(summed, train_norm)):
            rotated[:, pl.ds(step * train_batch + i, 1), :] = value[:, None, :]
        return carry

    def train_part(i):
        loads[i].wait()
        lax.fori_loop(i * per_part, (i + 1) * per_part, train_step, 0)

    batches = rows_own.shape[1]
    batch_docs = train_docs // batches

    def send_rows(i):
        rows_own[:, i] = rotated[:, i * batch_docs:(i + 1) * batch_docs, :].astype(BF16)

        for k in ring_steps:
            pltpu.make_async_remote_copy(
                src_ref=rows_own.at[pl.ds(y_at[k] * slab, slab), i],
                dst_ref=rows_all.at[:, y, i],
                send_sem=rows_sem.at[0],
                recv_sem=rows_sem.at[1],
                device_id=device(z, x_lo, x_hi, y_at[k]),
                device_id_type=MESH,
            ).start()
        rows_all[:, y, i] = rows_own[pl.ds(y * slab, slab), i]

    train_part(0)
    pair_copy.wait()
    sums = sibling_part[...] + partial[:, core]
    sums_ref[...] = sums.reshape(ny, 2, tile_rows, lanes).astype(BF16)

    def send_reduce(s, half, target):
        pltpu.make_async_remote_copy(
            src_ref=sums_ref.at[s, half],
            dst_ref=pieces.at[z * 2 + x_lo],
            send_sem=reduce_sem.at[0],
            recv_sem=reduce_sem.at[1],
            device_id=target,
            device_id_type=MESH,
        ).start()

    for k in ring_steps:
        for half in range(2):
            send_reduce(y_at[k], half, device(y, half, x_hi, y_at[k]))
    for half in range(2):
        itself = own_tile & (x_lo == half)

        @pl.when(itself)
        def _(half=half):
            src, dst = sums_ref.at[y, half], pieces.at[z * 2 + x_lo]
            pltpu.make_async_copy(src, dst, reduce_sem.at[1]).start()

        @pl.when(jnp.logical_not(itself))
        def _(half=half):
            send_reduce(y, half, device(y, half, x_hi, y))

    train_part(1)
    send_rows(0)
    train_part(2)
    train_part(3)
    send_rows(1)
    pltpu.make_async_copy(pieces, pieces, reduce_sem.at[1]).wait()
    total = pieces[0].astype(F32)
    for j in range(1, nz * 2):
        total = total + pieces[j].astype(F32)
    gathered[core, z * 4 + x_lo * 2 + x_hi] = total.astype(BF16)

    mine = gathered.at[core, z * 4 + x_lo * 2 + x_hi]
    def ranges(k):
        return int(hops(k, nz) > nz // 4)

    for k, m in plane_steps:
        pltpu.make_async_remote_copy(
            src_ref=mine,
            dst_ref=mine,
            send_sem=plane_sem.at[0],
            recv_sem=plane_sem.at[1 + ranges(k)],
            device_id=plane_partner(k, m),
            device_id_type=MESH,
        ).start()

    def forward(k):
        window = gathered.at[core, pl.ds(z_at[k] * 4, 4)]
        pltpu.make_async_remote_copy(
            src_ref=window,
            dst_ref=window,
            send_sem=sib_sem.at[0],
            recv_sem=sib_sem.at[1],
            device_id=sibling,
            device_id_type=MESH,
        ).start()

    for group in range(2):
        places = [k for k in range(nz) if ranges(k) == group]
        arrived = gathered.at[0, pl.ds(0, len(places) * 4 - (group == 0))]
        pltpu.make_async_copy(arrived, arrived, plane_sem.at[1 + group]).wait()
        for k in places:
            forward(k)
    received = rows_all.at[:, pl.ds(0, ny - 1)]
    pltpu.make_async_copy(received, received, rows_sem.at[1]).wait()

    ring_docs = ny * train_docs

    def product(side):
        queries, documents = [], []
        for xl in range(2):
            tiles = [gathered[side, i * 4 + xl * 2 + xh] for i in range(nz) for xh in range(2)]
            queries.append(jnp.concatenate(tiles, axis=0))
            row = side * (slab // 2) + xl * 2
            documents.append(rows_all[pl.ds(row, 2)].reshape(2 * ring_docs, lanes))
        result = lax.dot_general(
            jnp.concatenate(queries, axis=1), jnp.concatenate(documents, axis=1),
            (((1,), (1,)), ((), ())), preferred_element_type=F32,
        )
        result = result.reshape(groups, 2, query_docs, 2 * ring_docs)
        return (result[:, 0, :, :ring_docs] + result[:, 1, :, ring_docs:]) * score_norm

    first = product(core)
    half_tiles = gathered.at[0]
    pltpu.make_async_copy(half_tiles, half_tiles, sib_sem.at[1]).wait()
    scores = first + product(1 - core)
    width = ring_docs // 2
    score_send[...] = jnp.concatenate([scores[:, :, :width], scores[:, :, width:]], axis=1).astype(BF16)

    for k, m in score_steps:
        dxh, dy, target = score_partner(k, m)
        pltpu.make_async_remote_copy(
            src_ref=score_send.at[dy * 2 + dxh],
            dst_ref=score_recv.at[query],
            send_sem=score_sem.at[0],
            recv_sem=score_sem.at[1],
            device_id=target,
            device_id_type=MESH,
        ).start()
    score_recv[query] = score_send[y * 2 + x_hi]

    pltpu.make_async_copy(half_tiles, half_tiles, sib_sem.at[0]).wait()
    others = gathered.at[0, pl.ds(0, len(plane_steps))]
    pltpu.make_async_copy(others, others, plane_sem.at[0]).wait()
    pltpu.make_async_copy(received, received, rows_sem.at[0]).wait()
    sent = pieces.at[pl.ds(0, nz * 2 - 1)]

    @pl.when(own_tile)
    def _():
        pltpu.make_async_copy(sent, sent, reduce_sem.at[0]).wait()

    @pl.when(jnp.logical_not(own_tile))
    def _():
        pltpu.make_async_copy(pieces, pieces, reduce_sem.at[0]).wait()

    blocks = score_recv.at[pl.ds(0, groups - 1)]
    pltpu.make_async_copy(blocks, blocks, score_sem.at[1]).wait()
    for side in range(2):
        value = score_recv[side * ny].astype(F32)
        for k in range(1, ny):
            value = value + score_recv[side * ny + k].astype(F32)
        out_ref[:, side * ring_docs:side * ring_docs + width] = value[:query_docs]
        out_ref[:, side * ring_docs + width:(side + 1) * ring_docs] = value[query_docs:]
    pltpu.make_async_copy(blocks, blocks, score_sem.at[0]).wait()


def on_device(
    train_factors, train_lengths, query_factors, query_lengths, basis_out, basis_in, eigenvalues
):
    layer_count, rank, _ = basis_in.shape
    train_docs, _, slots, lanes = train_factors.shape
    query_docs = query_factors.shape[0]
    trains = lax.axis_size("train")
    groups = lax.axis_size("query")
    nz, ny = trains // 4, groups // 2
    slab = rank // ny
    tile_rows = 2 * query_docs
    batches = 2
    score_norm = 1.0 / (rank * math.sqrt(layer_count))
    train_norm = 1.0 / math.sqrt(slots)
    query_norm = 1.0 / math.sqrt(slots * trains)
    vmem = pl.BlockSpec(memory_space=pltpu.VMEM)
    hbm = pl.BlockSpec(memory_space=pltpu.HBM)
    dma = pltpu.SemaphoreType.DMA
    scores = pl.pallas_call(
        functools.partial(kernel, nz, ny, score_norm, train_norm, query_norm),
        out_shape=jax.ShapeDtypeStruct((query_docs, groups * train_docs), F32),
        in_specs=[hbm] * 7,
        out_specs=vmem,
        scratch_shapes=[
            pltpu.VMEM(train_factors.shape, BF16),
            pltpu.SMEM(train_lengths.shape, jnp.int32),
            pltpu.VMEM(query_factors.shape, BF16),
            pltpu.SMEM(query_lengths.shape, jnp.int32),
            pltpu.VMEM(basis_out.shape, F32),
            pltpu.VMEM(basis_in.shape, F32),
            pltpu.VMEM(eigenvalues.shape, F32),
            pltpu.VMEM((3 * lanes, lanes), BF16),
            pltpu.VMEM((lanes, 3 * rank), BF16),
            pltpu.VMEM((rank, lanes), F32),
            pltpu.VMEM((ny, 2, slab // 2, query_docs, lanes), F32),
            pltpu.VMEM((ny, slab // 2, query_docs, lanes), F32),
            pltpu.VMEM((ny, 2, tile_rows, lanes), BF16),
            pltpu.VMEM((nz * 2, tile_rows, lanes), BF16),
            pltpu.VMEM((2, nz * 4, tile_rows, lanes), BF16),
            pltpu.VMEM((rank, train_docs, lanes), F32),
            pltpu.VMEM((rank, batches, train_docs // batches, lanes), BF16),
            pltpu.VMEM((slab, ny, batches, train_docs // batches, lanes), BF16),
            pltpu.VMEM((groups, tile_rows, ny * train_docs // 2), BF16),
            pltpu.VMEM((groups, tile_rows, ny * train_docs // 2), BF16),
            dma((4,)),
            dma,
            dma((5,)),
            dma((2,)),
            dma((2,)),
            dma((nz // 2 + 2,)),
            dma((2,)),
            dma((2,)),
            dma((2,)),
        ],
        compiler_params=pltpu.CompilerParams(
            collective_id=0, has_side_effects=True, vmem_limit_bytes=64 * 1024 * 1024
        ),
        cost_estimate=pl.CostEstimate(flops=400_000_000, bytes_accessed=6_000_000, transcendentals=0),
    )(
        train_factors, train_lengths, query_factors, query_lengths, basis_out, basis_in, eigenvalues
    )
    return scores.T


def solution(mesh):
    return jax.shard_map(
        on_device,
        mesh=mesh,
        in_specs=(
            P(("train", "query"), None, None, None),
            P(("train", "query")),
            P("query", None, "train", None),
            P("query"),
            P(),
            P(),
            P(),
        ),
        out_specs=P("train", "query"),
        check_vma=False,
    )
```

```python
import functools
import math

import jax
import jax.numpy as jnp
from jax import lax
from jax.experimental import pallas as pl
from jax.experimental.pallas import tpu as pltpu
from jax.sharding import PartitionSpec as P

F32 = jnp.float32
BF16 = jnp.bfloat16
MESH = pl.DeviceIdType.MESH


def split(value):
    high = value.astype(BF16)
    return high, (value - high.astype(F32)).astype(BF16)


def mm(lhs, rhs):
    return jnp.dot(lhs, rhs, preferred_element_type=F32)


def kernel(
    nz, ny, score_norm, train_norm, query_norm,
    train_hbm, train_len_hbm, query_hbm, query_len_hbm, basis_out_hbm, basis_in_hbm, eigenvalues_hbm,
    out_ref,
    train_buf, train_len, query_buf, query_len, basis_out, basis_in, eigenvalues,
    right_ref, left_ref, scale_ref,
    partial, sibling_part, sums_ref, pieces, gathered, rotated, rows_own, rows_all, score_send, score_recv,
    load_sem, query_sem, small_sem, pair_sem, reduce_sem, plane_sem, sib_sem, rows_sem, score_sem,
):
    rank = basis_in.shape[1]
    lanes = 2 * rank
    train_docs = train_hbm.shape[0]
    query_docs = query_hbm.shape[0]
    slots = train_hbm.shape[2]
    slab = rank // ny
    groups = ny * 2
    plane = nz * 4
    tile_rows = 2 * query_docs

    train = lax.axis_index("train")
    query = lax.axis_index("query")
    z = train // 4
    x_lo = (train // 2) % 2
    core = train % 2
    x_hi = query // ny
    y = query % ny
    z_at = [lax.rem(z + k, nz) for k in range(nz)]
    y_at = [lax.rem(y + k, ny) for k in range(ny)]
    x_at = [(x_lo, x_hi), (1 - x_lo, x_hi), (x_lo, 1 - x_hi), (1 - x_lo, 1 - x_hi)]

    def hops(k, size):
        return min(k, size - k)

    plane_steps = [(k, m) for k in range(nz) for m in range(4) if k or m]
    plane_steps.sort(key=lambda step: -hops(step[0], nz) - (0, 1, 2, 1)[step[1]])
    score_steps = [(k, m) for k in range(ny) for m in range(2) if k or m]
    score_steps.sort(key=lambda step: -hops(step[0], ny) - 2 * step[1])
    ring_steps = sorted(range(1, ny), key=lambda k: -hops(k, ny))

    def device(dz, dxl, dxh, dy):
        return dz * 4 + dxl * 2 + core, dxh * ny + dy

    sibling = (train + 1 - 2 * core, query)

    def plane_partner(k, m):
        return device(z_at[k], x_at[m][0], x_at[m][1], y)

    def score_partner(k, m):
        dxh = 1 - x_hi if m else x_hi
        return dxh, y_at[k], (train, dxh * ny + y_at[k])

    load_query = pltpu.make_async_copy(query_hbm, query_buf, query_sem)
    load_query.start()
    small = [
        pltpu.make_async_copy(src, dst, small_sem.at[i])
        for i, (src, dst) in enumerate(
            [
                (query_len_hbm, query_len),
                (basis_in_hbm, basis_in),
                (basis_out_hbm, basis_out),
                (eigenvalues_hbm, eigenvalues),
                (train_len_hbm, train_len),
            ]
        )
    ]
    for copy in small:
        copy.start()
    barrier = pltpu.get_barrier_semaphore()

    def greet(target):
        pl.semaphore_signal(barrier, inc=1, device_id=target, device_id_type=MESH)

    own_tile = y == z
    for k in sorted(range(nz), key=lambda k: -hops(k, nz)):
        for half in range(2):
            source, group = device(z_at[k], half, x_hi, z)
            if k == 0:
                source = source + jnp.where(own_tile & (x_lo == half), 1 - 2 * core, 0)
            greet((source, group))
    for k, m in score_steps:
        greet(score_partner(k, m)[2])
    for k, m in plane_steps:
        greet(plane_partner(k, m))
    greet(sibling)
    greetings = 1 + nz * 2 + len(plane_steps) + len(score_steps)

    parts = load_sem.shape[0]
    part_docs = train_docs // parts
    loads = []
    for i in range(parts):
        window = pl.ds(i * part_docs, part_docs)
        loads.append(pltpu.make_async_copy(train_hbm.at[window], train_buf.at[window], load_sem.at[i]))
        loads[-1].start()

    for copy in small:
        copy.wait()
    zero = jnp.zeros((rank, rank), F32)
    block = jnp.concatenate(
        [
            jnp.concatenate([basis_in[0], zero], axis=1),
            jnp.concatenate([zero, basis_in[1]], axis=1),
        ],
        axis=0,
    )
    high, low = split(block)
    right_ref[...] = jnp.concatenate([high, high, low], axis=0)
    turned = jnp.concatenate([basis_out[0].T, basis_out[1].T], axis=0)
    high, low = split(turned)
    left_ref[...] = jnp.concatenate([high, high, low], axis=1)
    scale_ref[...] = 1.0 / jnp.sqrt(jnp.concatenate([eigenvalues[0], eigenvalues[1]], axis=1))

    lane = lax.broadcasted_iota(jnp.int32, (rank, lanes), 1)
    first_layer = lane < rank
    token = lax.broadcasted_iota(jnp.int32, (slots, lanes), 0)

    def outer(factors, live):
        mask = jnp.where(token < live, 1.0, 0.0).astype(BF16)
        sums = []
        for layer in range(2):
            tokens = factors[layer]
            masked = tokens * mask
            product = lax.dot_general(
                masked, tokens, (((0,), (0,)), ((), ())), preferred_element_type=F32
            )
            sums.append(product[rank:])
        return jnp.where(first_layer, sums[0], pltpu.roll(sums[1], rank, 1))

    def rotate(summed, norm):
        count = len(summed)
        high, low = split(jnp.concatenate(summed, axis=0))
        turned = mm(jnp.concatenate([high, low, high], axis=1), right_ref[...])
        high, low = split(turned)
        columns = []
        for i in range(count):
            rows = slice(i * rank, (i + 1) * rank)
            columns.append(jnp.concatenate([high[rows], low[rows], high[rows]], axis=0))
        product = mm(left_ref[...], jnp.concatenate(columns, axis=1))
        scale = scale_ref[...] * norm
        results = []
        for i in range(count):
            mine = product[:, i * lanes:(i + 1) * lanes]
            results.append(jnp.where(first_layer, mine[:rank], mine[rank:]) * scale)
        return results

    load_query.wait()
    query_batch = 8

    def query_step(step, carry):
        summed = []
        for i in range(query_batch):
            doc = step * query_batch + i
            summed.append(outer(query_buf[doc], query_len[doc] - train * slots))
        for i, value in enumerate(rotate(summed, query_norm)):
            partial[:, :, :, pl.ds(step * query_batch + i, 1), :] = value.reshape(ny, 2, slab // 2, 1, lanes)
        return carry

    lax.fori_loop(0, query_docs // query_batch, query_step, 0)

    pl.semaphore_wait(barrier, greetings)
    pair_copy = pltpu.make_async_remote_copy(
        src_ref=partial.at[:, 1 - core],
        dst_ref=sibling_part,
        send_sem=pair_sem.at[0],
        recv_sem=pair_sem.at[1],
        device_id=sibling,
        device_id_type=MESH,
    )
    pair_copy.start()

    train_batch = 4
    per_part = part_docs // train_batch

    def train_step(step, carry):
        summed = []
        for i in range(train_batch):
            doc = step * train_batch + i
            summed.append(outer(train_buf[doc], train_len[doc]))
        for i, value in enumerate(rotate(summed, train_norm)):
            rotated[:, pl.ds(step * train_batch + i, 1), :] = value[:, None, :]
        return carry

    def train_part(i):
        loads[i].wait()
        lax.fori_loop(i * per_part, (i + 1) * per_part, train_step, 0)

    batches = rows_own.shape[1]
    batch_docs = train_docs // batches

    def send_rows(i):
        rows_own[:, i] = rotated[:, i * batch_docs:(i + 1) * batch_docs, :].astype(BF16)

        for k in ring_steps:
            pltpu.make_async_remote_copy(
                src_ref=rows_own.at[pl.ds(y_at[k] * slab, slab), i],
                dst_ref=rows_all.at[:, y, i],
                send_sem=rows_sem.at[0],
                recv_sem=rows_sem.at[1],
                device_id=device(z, x_lo, x_hi, y_at[k]),
                device_id_type=MESH,
            ).start()
        rows_all[:, y, i] = rows_own[pl.ds(y * slab, slab), i]

    train_part(0)
    pair_copy.wait()
    sums = sibling_part[...] + partial[:, core]
    sums_ref[...] = sums.reshape(ny, 2, tile_rows, lanes).astype(BF16)

    def send_reduce(s, half, target):
        pltpu.make_async_remote_copy(
            src_ref=sums_ref.at[s, half],
            dst_ref=pieces.at[z * 2 + x_lo],
            send_sem=reduce_sem.at[0],
            recv_sem=reduce_sem.at[1],
            device_id=target,
            device_id_type=MESH,
        ).start()

    for k in ring_steps:
        for half in range(2):
            send_reduce(y_at[k], half, device(y, half, x_hi, y_at[k]))
    for half in range(2):
        itself = own_tile & (x_lo == half)

        @pl.when(itself)
        def _(half=half):
            src, dst = sums_ref.at[y, half], pieces.at[z * 2 + x_lo]
            pltpu.make_async_copy(src, dst, reduce_sem.at[1]).start()

        @pl.when(jnp.logical_not(itself))
        def _(half=half):
            send_reduce(y, half, device(y, half, x_hi, y))

    train_part(1)
    send_rows(0)
    train_part(2)
    train_part(3)
    send_rows(1)
    pltpu.make_async_copy(pieces, pieces, reduce_sem.at[1]).wait()
    total = pieces[0].astype(F32)
    for j in range(1, nz * 2):
        total = total + pieces[j].astype(F32)
    gathered[core, z * 4 + x_lo * 2 + x_hi] = total.astype(BF16)

    mine = gathered.at[core, z * 4 + x_lo * 2 + x_hi]
    def ranges(k):
        return int(hops(k, nz) > nz // 4)

    for k, m in plane_steps:
        pltpu.make_async_remote_copy(
            src_ref=mine,
            dst_ref=mine,
            send_sem=plane_sem.at[0],
            recv_sem=plane_sem.at[1 + ranges(k)],
            device_id=plane_partner(k, m),
            device_id_type=MESH,
        ).start()

    def forward(k):
        window = gathered.at[core, pl.ds(z_at[k] * 4, 4)]
        pltpu.make_async_remote_copy(
            src_ref=window,
            dst_ref=window,
            send_sem=sib_sem.at[0],
            recv_sem=sib_sem.at[1],
            device_id=sibling,
            device_id_type=MESH,
        ).start()

    for group in range(2):
        places = [k for k in range(nz) if ranges(k) == group]
        arrived = gathered.at[0, pl.ds(0, len(places) * 4 - (group == 0))]
        pltpu.make_async_copy(arrived, arrived, plane_sem.at[1 + group]).wait()
        for k in places:
            forward(k)
    received = rows_all.at[:, pl.ds(0, ny - 1)]
    pltpu.make_async_copy(received, received, rows_sem.at[1]).wait()

    ring_docs = ny * train_docs

    def product(side, steps):
        queries, documents = [], []
        for xl in range(2):
            tiles = []
            for k, m in steps:
                dxh, dy, _ = score_partner(k, m)
                tiles.append(gathered[side, dy * 4 + xl * 2 + dxh])
            queries.append(jnp.concatenate(tiles, axis=0))
            row = side * (slab // 2) + xl * 2
            documents.append(rows_all[pl.ds(row, 2)].reshape(2 * ring_docs, lanes))
        result = lax.dot_general(
            jnp.concatenate(queries, axis=1), jnp.concatenate(documents, axis=1),
            (((1,), (1,)), ((), ())), preferred_element_type=F32,
        )
        result = result.reshape(len(steps), 2, query_docs, 2 * ring_docs)
        return (result[:, 0, :, :ring_docs] + result[:, 1, :, ring_docs:]) * score_norm

    all_steps = score_steps + [(0, 0)]
    step_halves = [all_steps[:groups // 2], all_steps[groups // 2:]]
    firsts = [product(core, steps) for steps in step_halves]
    half_tiles = gathered.at[0]
    pltpu.make_async_copy(half_tiles, half_tiles, sib_sem.at[1]).wait()
    width = ring_docs // 2
    for part, steps in enumerate(step_halves):
        scores = firsts[part] + product(1 - core, steps)
        slot = part * (groups // 2)
        score_send[slot:slot + len(steps)] = jnp.concatenate(
            [scores[:, :, :width], scores[:, :, width:]], axis=1
        ).astype(BF16)
        for i, (k, m) in enumerate(steps):
            if k == 0 and m == 0:
                score_recv[query] = score_send[slot + i]
                continue
            pltpu.make_async_remote_copy(
                src_ref=score_send.at[slot + i],
                dst_ref=score_recv.at[query],
                send_sem=score_sem.at[0],
                recv_sem=score_sem.at[1],
                device_id=score_partner(k, m)[2],
                device_id_type=MESH,
            ).start()

    pltpu.make_async_copy(half_tiles, half_tiles, sib_sem.at[0]).wait()
    others = gathered.at[0, pl.ds(0, len(plane_steps))]
    pltpu.make_async_copy(others, others, plane_sem.at[0]).wait()
    pltpu.make_async_copy(received, received, rows_sem.at[0]).wait()
    sent = pieces.at[pl.ds(0, nz * 2 - 1)]

    @pl.when(own_tile)
    def _():
        pltpu.make_async_copy(sent, sent, reduce_sem.at[0]).wait()

    @pl.when(jnp.logical_not(own_tile))
    def _():
        pltpu.make_async_copy(pieces, pieces, reduce_sem.at[0]).wait()

    blocks = score_recv.at[pl.ds(0, groups - 1)]
    pltpu.make_async_copy(blocks, blocks, score_sem.at[1]).wait()
    for side in range(2):
        value = score_recv[side * ny].astype(F32)
        for k in range(1, ny):
            value = value + score_recv[side * ny + k].astype(F32)
        out_ref[:, side * ring_docs:side * ring_docs + width] = value[:query_docs]
        out_ref[:, side * ring_docs + width:(side + 1) * ring_docs] = value[query_docs:]
    pltpu.make_async_copy(blocks, blocks, score_sem.at[0]).wait()


def on_device(
    train_factors, train_lengths, query_factors, query_lengths, basis_out, basis_in, eigenvalues
):
    layer_count, rank, _ = basis_in.shape
    train_docs, _, slots, lanes = train_factors.shape
    query_docs = query_factors.shape[0]
    trains = lax.axis_size("train")
    groups = lax.axis_size("query")
    nz, ny = trains // 4, groups // 2
    slab = rank // ny
    tile_rows = 2 * query_docs
    batches = 2
    score_norm = 1.0 / (rank * math.sqrt(layer_count))
    train_norm = 1.0 / math.sqrt(slots)
    query_norm = 1.0 / math.sqrt(slots * trains)
    vmem = pl.BlockSpec(memory_space=pltpu.VMEM)
    hbm = pl.BlockSpec(memory_space=pltpu.HBM)
    dma = pltpu.SemaphoreType.DMA
    scores = pl.pallas_call(
        functools.partial(kernel, nz, ny, score_norm, train_norm, query_norm),
        out_shape=jax.ShapeDtypeStruct((query_docs, groups * train_docs), F32),
        in_specs=[hbm] * 7,
        out_specs=vmem,
        scratch_shapes=[
            pltpu.VMEM(train_factors.shape, BF16),
            pltpu.SMEM(train_lengths.shape, jnp.int32),
            pltpu.VMEM(query_factors.shape, BF16),
            pltpu.SMEM(query_lengths.shape, jnp.int32),
            pltpu.VMEM(basis_out.shape, F32),
            pltpu.VMEM(basis_in.shape, F32),
            pltpu.VMEM(eigenvalues.shape, F32),
            pltpu.VMEM((3 * lanes, lanes), BF16),
            pltpu.VMEM((lanes, 3 * rank), BF16),
            pltpu.VMEM((rank, lanes), F32),
            pltpu.VMEM((ny, 2, slab // 2, query_docs, lanes), F32),
            pltpu.VMEM((ny, slab // 2, query_docs, lanes), F32),
            pltpu.VMEM((ny, 2, tile_rows, lanes), BF16),
            pltpu.VMEM((nz * 2, tile_rows, lanes), BF16),
            pltpu.VMEM((2, nz * 4, tile_rows, lanes), BF16),
            pltpu.VMEM((rank, train_docs, lanes), F32),
            pltpu.VMEM((rank, batches, train_docs // batches, lanes), BF16),
            pltpu.VMEM((slab, ny, batches, train_docs // batches, lanes), BF16),
            pltpu.VMEM((groups, tile_rows, ny * train_docs // 2), BF16),
            pltpu.VMEM((groups, tile_rows, ny * train_docs // 2), BF16),
            dma((4,)),
            dma,
            dma((5,)),
            dma((2,)),
            dma((2,)),
            dma((nz // 2 + 2,)),
            dma((2,)),
            dma((2,)),
            dma((2,)),
        ],
        compiler_params=pltpu.CompilerParams(
            collective_id=0, has_side_effects=True, vmem_limit_bytes=64 * 1024 * 1024
        ),
        cost_estimate=pl.CostEstimate(flops=400_000_000, bytes_accessed=6_000_000, transcendentals=0),
    )(
        train_factors, train_lengths, query_factors, query_lengths, basis_out, basis_in, eigenvalues
    )
    return scores.T


def solution(mesh):
    return jax.shard_map(
        on_device,
        mesh=mesh,
        in_specs=(
            P(("train", "query"), None, None, None),
            P(("train", "query")),
            P("query", None, "train", None),
            P("query"),
            P(),
            P(),
            P(),
        ),
        out_specs=P("train", "query"),
        check_vma=False,
    )
```
